256 devices in a mesh: expert: 32 (over y_hi, z, core), dp: 8 (over x, y_lo).
Axes of the slice: x: 4, y: 4 (y_hi: 2, y_lo: 2; y = y_hi * 2 + y_lo), z: 8, core: 2. Of those that a mesh axis runs over, the one named last changes fastest.
Arguments:
- tokens: bfloat16 [2, 512, 3584], P(None, 'expert', 'dp'), may hold values from -6 to 6
- routes: int32 [2, 512, 8], P(None, 'expert'), may hold values from 0 to 63, all different within a row; in each aligned block of 16 rows (0 to 15, 16 to 31, ..., all dimensions but the last counted through in order) at most 4 rows name the same one
- gate_fix: int32 [2, 512, 8], P(None, 'expert'), may hold values from 1 to 65535
- position: int32 [64], replicated, may hold values from 0 to 63, each once
- swap_slot: int32 [32], replicated, may hold values from 0 to 1
- w_gate: bfloat16 [64, 3584, 1024], P('expert', None, 'dp'), may hold values from -0.09375 to 0.09375
- w_up: bfloat16 [64, 3584, 1024], P('expert', None, 'dp'), may hold values from -0.09375 to 0.09375
- w_down: bfloat16 [64, 1024, 3584], P('expert', 'dp'), may hold values from -0.1875 to 0.1875
Outputs:
- combined: bfloat16 [2, 512, 3584], P(None, 'expert', 'dp')
- device_load: float32 [32], P('expert')
- swapped_gate: bfloat16 [64, 3584, 1024], P('expert', None, 'dp')
- swapped_up: bfloat16 [64, 3584, 1024], P('expert', None, 'dp')
- swapped_down: bfloat16 [64, 1024, 3584], P('expert', 'dp')
The draws below stay inside these ranges and needn't reach their ends.
Inputs may be any that keep to these rules, and one draw needn't show every extreme that they name: `routes`: in each step the 16 tokens of one index of expert name any one expert in at most 4 rows, and in some such block one expert is named by exactly 4. `position`: each expert once.
All inputs are finite; a program needn't handle non-finite values.
Results may differ from the reference program's by a relative error of at most 0.02.
Values may be sent and summed in bfloat16 or wider, within the bound.
No kernel may reach another device: no remote copies, remote signals or barrier semaphores. Data moves between devices by JAX's collectives and lax.ppermute only.
A program may use at most 128 MiB of HBM per device.

```python
import math
import jax
import jax.numpy as jnp
import numpy as np
from jax import lax

D = 3584
FF = 1024
TOPK = 8
EXP_LOC = 2
STEPS = 2
TOK_GRP = 16
EXPERTS = 64
TOKENS = 512
CAP = 4
N_EXPERT = 32
N_DP = 8


def plant(drawn, stream_key, low, top_value):
    dims = drawn.shape
    spot = [jax.random.randint(jax.random.fold_in(stream_key, axis), (), 0, dims[axis]) for axis in range(len(dims))]
    drawn = drawn.at[tuple(spot)].set(low)
    longest = dims.index(max(dims))
    spot[longest] = (spot[longest] + 1) % dims[longest]
    return drawn.at[tuple(spot)].set(top_value)


def levels(key, shape, split, least, largest):
    factor_of = 1.0
    for dim, blocks in split:
        steps = jax.random.uniform(jax.random.fold_in(jax.random.fold_in(key, 6), dim), (blocks,), jnp.float32, least / len(split), largest / len(split))
        factor_of = factor_of * jnp.repeat(jnp.exp(steps), shape[dim] // blocks).reshape((-1,) + (1,) * (len(shape) - 1 - dim))
    return factor_of


def deal_out(stream_key, own, number, rows, count, top, limit, skew):
    order = jax.random.permutation(stream_key, count)
    crowded, ordinary = load_shares(count, rows * top, limit, skew, True), load_shares(count, rows * top, limit, skew, False)
    places = jnp.arange(count)

    def named(sizes, rotation):
        used = int((sizes > 0).sum())
        fixed = max(1, used // 4)
        moved = fixed + (places - fixed + rotation * (used - fixed)) % max(1, count - fixed)
        return jnp.zeros((count,), jnp.int32).at[order[jnp.where(places < fixed, places, moved)]].set(jnp.asarray(sizes, jnp.int32))

    sizes = jnp.where(number % 4 == 0, named(crowded, number // 4), named(ordinary, number - number // 4 - 1))
    mixed = jax.random.permutation(jax.random.fold_in(own, 3), count)
    source_of, taker = mixed[0:count // 2 * 2:2], mixed[1:count // 2 * 2:2]
    slack = jnp.minimum(sizes[source_of] - 1, limit - sizes[taker]) // 2
    slack = jnp.where((source_of == order[0]) | (taker == order[0]) | (sizes[taker] == 0), 0, jnp.maximum(slack, 0))
    moved = jax.random.randint(jax.random.fold_in(own, 4), (count // 2,), 0, 1 << 20) % (slack + 1)
    sizes = sizes.at[source_of].add(-moved).at[taker].add(moved)
    items = jnp.searchsorted(jnp.cumsum(sizes), jnp.arange(rows * top), side="right").astype(jnp.int32)
    listing = items.reshape(top, rows).T
    listing = listing[jax.random.permutation(jax.random.fold_in(own, 1), rows)]
    rotation = jax.random.randint(jax.random.fold_in(own, 2), (rows, 1), 0, top)
    return jnp.take_along_axis(listing, (jnp.arange(top)[None, :] + rotation) % top, axis=1)


def load_shares(count, total, reach, lean, full):
    portions = [(1 << 20) // math.isqrt(standing ** lean) + 1 for standing in range(1, count + 1)]
    largest = reach if full else min(reach, max(-(-total // count), total * portions[0] // sum(portions)))
    least = 1 if total - largest >= count - 1 else 0
    counts, rest = [largest] + [least] * (count - 1), total - largest - least * (count - 1)
    while rest > 0:
        free = [i for i in range(1, count) if counts[i] < largest] or [i for i in range(1, count) if counts[i] < reach]
        mass, budget = sum([portions[i] for i in free]), rest
        for i in free:
            more = min(reach - counts[i], max(1, budget * portions[i] // mass), rest)
            counts[i] = counts[i] + more
            rest = rest - more
    return np.array(counts)


def scatter_about(own_key, dims, deviation, reach, split=(), kind=jnp.bfloat16):
    level = levels(own_key, dims, split, -0.22, 0.18) if split else 1.0
    entries = jax.random.normal(own_key, dims, jnp.float32) * deviation * level
    return jnp.minimum(jnp.maximum(entries, -reach), reach).astype(kind)


def setup_inputs(seed: int = 0) -> dict:
    streams_of = jax.random.split(jax.random.key(seed), 9)
    tokens = scatter_about(streams_of[0], (STEPS, TOKENS, D), 1.0, 6.0, ((1, 32), (2, 8)))
    routes_keys = jax.random.split(jax.random.fold_in(streams_of[1], 1), STEPS * TOKENS // TOK_GRP)
    routes_turns = jax.random.permutation(jax.random.fold_in(streams_of[1], 3), STEPS * TOKENS // TOK_GRP)
    routes = jax.vmap(lambda own, number: deal_out(jax.random.fold_in(streams_of[1], 2), own, number, TOK_GRP, EXPERTS, TOPK, CAP, 2))(routes_keys, routes_turns).reshape((STEPS, TOKENS, TOPK))
    gate_fix = plant(jax.random.randint(streams_of[2], (STEPS, TOKENS, TOPK), 1, 65536), jax.random.fold_in(streams_of[2], 1), 1, 65535).astype(jnp.int32)
    position = jax.random.permutation(streams_of[3], EXPERTS).astype(jnp.int32)
    swap_slot = plant(jax.random.randint(streams_of[4], (N_EXPERT,), 0, EXP_LOC), jax.random.fold_in(streams_of[4], 1), 0, EXP_LOC - 1).astype(jnp.int32)
    w_gate = scatter_about(streams_of[5], (EXPERTS, D, FF), D ** -0.5, 0.09375, ((0, 32), (2, 8)))
    w_up = scatter_about(streams_of[6], (EXPERTS, D, FF), D ** -0.5, 0.09375, ((0, 32), (2, 8)))
    w_down = scatter_about(streams_of[7], (EXPERTS, FF, D), FF ** -0.5, 0.1875, ((0, 32), (1, 8)))
    return {"tokens": tokens, "routes": routes, "gate_fix": gate_fix, "position": position, "swap_slot": swap_slot, "w_gate": w_gate, "w_up": w_up, "w_down": w_down}


def lookup(keys, values_table, count):
    labels = jnp.arange(count, dtype=jnp.int32)
    return jnp.sum(jnp.where(keys[..., None] == labels, values_table, 0), axis=-1).astype(jnp.int32)


def ranks_of(expert_ids):
    labels = jnp.arange(EXPERTS, dtype=jnp.int32)
    named_count = jnp.sum((expert_ids[:, :, None] == labels).astype(jnp.int32), axis=1)
    before = jnp.cumsum(named_count, axis=0) - named_count
    return jnp.sum(jnp.where(expert_ids[:, :, None] == labels, before[:, None, :], 0), axis=2).astype(jnp.int32)


def relocate(stored, swap_slot):
    holder = (stored // EXP_LOC).astype(jnp.int32)
    held_slot = (stored % EXP_LOC).astype(jnp.int32)
    partner = jnp.bitwise_xor(holder, N_EXPERT // 2).astype(jnp.int32)
    return jnp.where(held_slot == lookup(holder, swap_slot, N_EXPERT),
                     partner * EXP_LOC + lookup(partner, swap_slot, N_EXPERT), stored).astype(jnp.int32)


def one_step(step_tokens, expert_ids, fixed_gates, position, w_gate, w_up, w_down):
    arrival = jax.vmap(ranks_of)(expert_ids.reshape(N_EXPERT, TOK_GRP, TOPK)).reshape(TOKENS, TOPK)
    token_index = jnp.broadcast_to(jnp.arange(TOKENS, dtype=jnp.int32)[:, None], (TOKENS, TOPK))
    anchor = (token_index // TOK_GRP).astype(jnp.int32)
    slot_table = jnp.full((EXPERTS, N_EXPERT, CAP), TOKENS, jnp.int32).at[expert_ids, anchor, arrival].set(token_index)
    padded = jnp.concatenate([step_tokens, jnp.zeros((1, D), step_tokens.dtype)], axis=0)

    def run_expert(expert):
        gathered = padded[slot_table[expert].reshape(-1)]
        stored = position[expert]
        gate_act = jnp.dot(gathered, w_gate[stored], preferred_element_type=jnp.float32)
        up_act = jnp.dot(gathered, w_up[stored], preferred_element_type=jnp.float32)
        hidden = (jax.nn.silu(gate_act) * up_act).astype(jnp.bfloat16)
        hidden_parts = hidden.reshape(-1, N_DP, FF // N_DP).astype(jnp.float32)
        down_panel = w_down[stored].reshape(N_DP, FF // N_DP, D).astype(jnp.float32)
        partial_value = jnp.einsum("rpf,pfd->prd", hidden_parts, down_panel).astype(jnp.bfloat16)
        partial_value = lax.optimization_barrier(partial_value)
        return jnp.sum(partial_value.astype(jnp.float32), axis=0).astype(jnp.bfloat16)

    expert_out = lax.map(run_expert, jnp.arange(EXPERTS, dtype=jnp.int32))
    selected = expert_out.reshape(EXPERTS, N_EXPERT, CAP, D)[expert_ids, anchor, arrival]
    gate_values = fixed_gates.astype(jnp.float32) / 65536.0
    return jnp.sum(gate_values[:, :, None] * selected.astype(jnp.float32), axis=1).astype(jnp.bfloat16)


def reference(tokens, routes, gate_fix, position, swap_slot, w_gate, w_up, w_down):
    moved = relocate(position, swap_slot)
    source = relocate(jnp.arange(EXPERTS, dtype=jnp.int32), swap_slot)
    swapped_gate = w_gate[source]
    swapped_up = w_up[source]
    swapped_down = w_down[source]
    combined = jnp.stack([one_step(tokens[decode_step], routes[decode_step], gate_fix[decode_step], position, w_gate, w_up, w_down)
                          for decode_step in range(STEPS)])
    new_holder = (lookup(routes[STEPS - 1], moved, EXPERTS) // EXP_LOC).astype(jnp.int32)
    counted = jnp.sum((new_holder[:, :, None] == jnp.arange(N_EXPERT, dtype=jnp.int32)).astype(jnp.float32), axis=(0, 1))
    device_load = counted / float(TOK_GRP * TOPK)
    return combined, device_load, swapped_gate, swapped_up, swapped_down
```

```python
import functools

import jax
import jax.numpy as jnp
import numpy as np
from jax import lax
from jax.experimental import pallas as pl
from jax.experimental.pallas import tpu as pltpu
from jax.sharding import Mesh, PartitionSpec as P

SIZES = {"yh": 2, "z": 8, "core": 2, "x": 4, "yl": 2}
EXPERT_AXES = ("yh", "z", "core")
DP_AXES = ("x", "yl")
GROUP = 16
WIDTH = 448
LANES = 512


def shift_pairs(axes, amount):
    count = int(np.prod([SIZES[a] for a in axes]))
    return [(i, (i + amount) % count) for i in range(count)]


def send(value, axes, amount):
    if amount == 0:
        return value
    return lax.ppermute(value, axes, shift_pairs(axes, amount))


Y = ("yh", "yl")
X = ("x",)
Z = ("z",)


def ring_size(axes):
    return int(np.prod([SIZES[a] for a in axes]))


def gather_ring(value, axes):
    return [send(value, axes, k) for k in range(ring_size(axes))]


def reduce_ring(pieces, axes):
    arrived = [send(piece, axes, -k) for k, piece in enumerate(pieces)]
    return functools.reduce(jnp.add, [a.astype(jnp.float32) for a in arrived]).astype(jnp.bfloat16)


def layer_kernel(z_last, *refs):
    n_pieces = 8 if z_last else 4
    place, position_ref = refs[:2]
    pieces = refs[2 : 2 + n_pieces]
    gate_own, up_own, down_own, gate_other, up_other, down_other = refs[2 + n_pieces : 8 + n_pieces]
    outs = refs[8 + n_pieces : 8 + 2 * n_pieces]
    count_ref = refs[8 + 2 * n_pieces]
    rows_ref, act_ref, result_ref = refs[9 + 2 * n_pieces :]
    my_x, my_y, my_core, chip = place[0], place[1], place[2], place[3]

    def spots():
        for zr in range(8):
            for xr in range(4):
                for yr in range(4):
                    first, second = (zr, xr) if z_last else (xr, zr)
                    x_at = lax.rem(my_x - xr + 4, 4)
                    y_at = lax.rem(my_y - yr + 4, 4)
                    block = x_at * 2 + lax.rem(y_at, 2)
                    row = pl.multiple_of((zr * 2 + lax.div(y_at, 2)) * GROUP, GROUP)
                    yield first, second, yr, block, row

    for first, second, yr, block, row in spots():
        rows_ref[block, pl.ds(row, GROUP), :] = pieces[first][second, yr]

    gates = rows_ref[0, :, WIDTH:].astype(jnp.float32) * 256.0 + rows_ref[1, :, WIDTH:].astype(jnp.float32)
    count_ref[...] = jnp.broadcast_to(
        jnp.sum((gates > 0.0).astype(jnp.float32), axis=0, keepdims=True), count_ref.shape
    )
    positions = position_ref[...]
    hidden = []
    for index, (gate_w, up_w, core) in enumerate(((gate_own, up_own, my_core), (gate_other, up_other, 1 - my_core))):
        for slot in range(2):
            stored = chip * 4 + core * 2 + slot
            share = jnp.sum(jnp.where(positions == stored, gates, 0.0), axis=1, keepdims=True) * (1.0 / 65536.0)
            act_ref[...] = jnp.zeros_like(act_ref)

            @pl.loop(0, 8)
            def _(block):
                at = pl.ds(pl.multiple_of(block * WIDTH, WIDTH), WIDTH)
                panel = jnp.concatenate([gate_w[slot, at, :], up_w[slot, at, :]], axis=1)
                act_ref[...] += jnp.dot(rows_ref[block, :, :WIDTH], panel, preferred_element_type=jnp.float32)

            gate_act, up_act = act_ref[:, :128], act_ref[:, 128:]
            hidden.append((jax.nn.silu(gate_act) * up_act * share).astype(jnp.bfloat16))
    hidden = jnp.concatenate(hidden, axis=1)
    for x_at in range(4):
        at = slice(x_at * 2 * WIDTH, (x_at + 1) * 2 * WIDTH)
        panel = jnp.concatenate(
            [down_own[0, :, at], down_own[1, :, at], down_other[0, :, at], down_other[1, :, at]], axis=0
        )
        part = jnp.dot(hidden, panel, preferred_element_type=jnp.float32)
        result_ref[2 * x_at] = part[:, :WIDTH].astype(jnp.bfloat16)
        result_ref[2 * x_at + 1] = part[:, WIDTH:].astype(jnp.bfloat16)

    for first, second, yr, block, row in spots():
        outs[first][second, yr] = result_ref[block, pl.ds(row, GROUP), :]


def run_layer(z_last, place, position, pieces, weights):
    vmem = pl.BlockSpec(memory_space=pltpu.VMEM)
    shape = pieces[0].shape[:-1] + (WIDTH,)
    out = pl.pallas_call(
        functools.partial(layer_kernel, z_last),
        out_shape=[jax.ShapeDtypeStruct(shape, jnp.bfloat16)] * len(pieces)
        + [jax.ShapeDtypeStruct((8, 64), jnp.float32)],
        in_specs=[pl.BlockSpec(memory_space=pltpu.SMEM)] + [vmem] * (1 + len(pieces) + 6),
        out_specs=[vmem] * (len(pieces) + 1),
        scratch_shapes=[
            pltpu.VMEM((8, 256, LANES), jnp.bfloat16),
            pltpu.VMEM((256, 256), jnp.float32),
            pltpu.VMEM((8, 256, WIDTH), jnp.bfloat16),
        ],
        compiler_params=pltpu.CompilerParams(vmem_limit_bytes=40 * 2**20),
        cost_estimate=pl.CostEstimate(flops=2 * 256 * 3584 * 1536, bytes_accessed=16 * 2**20, transcendentals=0),
        name="layer_z_last" if z_last else "layer_x_last",
    )(place, position, *pieces, *weights)
    return out[:-1], out[-1]


def on_device(tokens, routes, gate_fix, position, swap_slot, w_gate, w_up, w_down):
    yh, z, core = (lax.axis_index(a) for a in EXPERT_AXES)
    x, yl = (lax.axis_index(a) for a in DP_AXES)
    own_index = (yh * 8 + z) * 2 + core
    place = jnp.stack([x, yh * 2 + yl, core, yh * 8 + z]).astype(jnp.int32)

    labels = jnp.arange(64, dtype=jnp.int32)
    part = jnp.where(yl == 0, gate_fix >> 8, (gate_fix & 255) + 0)
    ride = jnp.sum(jnp.where(routes[..., None] == labels, part[..., None], 0), axis=2).astype(jnp.bfloat16)
    lower = jnp.concatenate([tokens, ride], axis=2)

    from_y = gather_ring(lower, Y)
    step_rows = [jnp.stack([v[s] for v in from_y]) for s in range(2)]

    swap_core = [(0, 1), (1, 0)]
    other = tuple(lax.ppermute(w, "core", swap_core) for w in (w_gate, w_up, w_down))
    weights = (w_gate, w_up, w_down) + other

    given_slot = lax.dynamic_index_in_dim(swap_slot, own_index, 0, keepdims=False)
    given = [lax.dynamic_index_in_dim(w, given_slot, 0, keepdims=False) for w in (w_gate, w_up, w_down)]
    given, step_rows = lax.optimization_barrier((given, step_rows))
    taken = [lax.ppermute(g, "yh", [(0, 1), (1, 0)]) for g in given]

    pieces0 = gather_ring(jnp.stack(gather_ring(step_rows[0], X)), Z)
    pieces1 = gather_ring(jnp.stack(gather_ring(step_rows[1], Z)), X)
    positions = position.reshape(1, 64)
    out0, _ = run_layer(True, place, positions, pieces0, weights)
    out1, counts = run_layer(False, place, positions, pieces1, weights)

    back0 = reduce_ring(out0, Z)
    back0 = reduce_ring([back0[k] for k in range(4)], X)
    back1 = reduce_ring(out1, X)
    back1 = reduce_ring([back1[k] for k in range(8)], Z)
    combined = reduce_ring([jnp.stack([back0[k], back1[k]]) for k in range(4)], Y)

    counts = counts[0] + lax.ppermute(counts[0], "core", swap_core)
    holder, held_slot = position // 2, position % 2
    partner = jnp.bitwise_xor(holder, 16)
    owners = jnp.arange(32, dtype=jnp.int32)
    slot_of = lambda h: jnp.sum(jnp.where(h[:, None] == owners, swap_slot, 0), axis=1)
    new_holder = jnp.where(held_slot == slot_of(holder), partner, holder)
    device_load = (jnp.sum(jnp.where(new_holder == own_index, counts, 0.0)) / 128.0).reshape(1)

    new = [lax.dynamic_update_index_in_dim(w, t, given_slot, 0) for w, t in zip((w_gate, w_up, w_down), taken)]
    return (combined, device_load, *new)


def solution(mesh):
    names = tuple(SIZES)
    fine = Mesh(mesh.devices.reshape(tuple(SIZES.values())), names)
    in_specs = (
        P(None, EXPERT_AXES, DP_AXES),
        P(None, EXPERT_AXES, None),
        P(None, EXPERT_AXES, None),
        P(),
        P(),
        P(EXPERT_AXES, None, DP_AXES),
        P(EXPERT_AXES, None, DP_AXES),
        P(EXPERT_AXES, DP_AXES, None),
    )
    out_specs = (
        P(None, EXPERT_AXES, DP_AXES),
        P(EXPERT_AXES),
        P(EXPERT_AXES, None, DP_AXES),
        P(EXPERT_AXES, None, DP_AXES),
        P(EXPERT_AXES, DP_AXES, None),
    )
    return jax.shard_map(on_device, mesh=fine, in_specs=in_specs, out_specs=out_specs, check_vma=False)
```

```python
import functools

import jax
import jax.numpy as jnp
import numpy as np
from jax import lax
from jax.experimental import pallas as pl
from jax.experimental.pallas import tpu as pltpu
from jax.sharding import Mesh, PartitionSpec as P

SIZES = {"yh": 2, "z": 8, "core": 2, "x": 4, "yl": 2}
EXPERT_AXES = ("yh", "z", "core")
DP_AXES = ("x", "yl")
Y = ("yh", "yl")
GROUP = 16
WIDTH = 448
PAIR = 2 * WIDTH
LANES = 512
SMALL = pltpu.CompilerParams(vmem_limit_bytes=4 * 2**20)


def ring_size(axes):
    return int(np.prod([SIZES[a] for a in axes]))


def send(value, axes, amount):
    count = ring_size(axes)
    return lax.ppermute(value, axes, [(i, (i + amount) % count) for i in range(count)])


def total(values):
    return functools.reduce(jnp.add, [v.astype(jnp.float32) for v in values]).astype(jnp.bfloat16)


def gather_ring(value, axes):
    return [value] + [send(value, axes, k) for k in range(1, ring_size(axes))]


def reduce_ring(pieces, axes):
    return total([pieces[0]] + [send(piece, axes, -k) for k, piece in enumerate(pieces) if k])


def gather_z(value):
    back, ahead, far = send(value, "z", 1), send(value, "z", -1), send(value, "z", 4)
    back2 = send(jnp.stack([value, back]), "z", 2)
    ahead2 = send(jnp.stack([value, ahead]), "z", -2)
    return run_join([value[None], back[None], back2, far[None], ahead2, ahead[None]])


def run_join(parts):
    vmem = pl.BlockSpec(memory_space=pltpu.VMEM)

    def join_kernel(*refs):
        at = 0
        for ref in refs[:-1]:
            refs[-1][at : at + ref.shape[0]] = ref[...]
            at += ref.shape[0]

    count = sum(p.shape[0] for p in parts)
    return pl.pallas_call(
        join_kernel,
        out_shape=jax.ShapeDtypeStruct((count,) + parts[0].shape[1:], parts[0].dtype),
        in_specs=[vmem] * len(parts),
        out_specs=vmem,
        compiler_params=SMALL,
        name="join",
    )(*parts)


def reduce_z(pieces):
    back2 = send(pieces[2:4], "z", -2)
    ahead2 = send(pieces[5:7], "z", 2)
    far = send(pieces[4], "z", -4)
    back = send(total([pieces[1], back2[1]]), "z", -1)
    ahead = send(total([pieces[7], ahead2[1]]), "z", 1)
    return total([pieces[0], back2[0], ahead2[0], far, back, ahead])


def ride_kernel(place, tokens_ref, routes_ref, gate_ref, out_ref):
    labels = lax.broadcasted_iota(jnp.int32, (2, GROUP, LANES - WIDTH), 2)
    gate = gate_ref[...]
    part = jnp.where(lax.rem(place[3], 2) == 0, gate >> 8, gate & 255)
    routes = routes_ref[...]
    ride = jnp.zeros(labels.shape, jnp.int32)
    for k in range(routes.shape[2]):
        ride = ride + jnp.where(routes[:, :, k : k + 1] == labels, part[:, :, k : k + 1], 0)
    ride = ride.astype(jnp.float32).astype(jnp.bfloat16)
    out_ref[...] = jnp.concatenate([tokens_ref[...], ride], axis=2)


def run_ride(place, tokens, routes, gate_fix):
    vmem = pl.BlockSpec(memory_space=pltpu.VMEM)
    return pl.pallas_call(
        ride_kernel,
        out_shape=jax.ShapeDtypeStruct((2, GROUP, LANES), jnp.bfloat16),
        in_specs=[pl.BlockSpec(memory_space=pltpu.SMEM)] + [vmem] * 3,
        out_specs=vmem,
        compiler_params=SMALL,
        name="ride",
    )(place, tokens, routes, gate_fix)


def merge_kernel(place, *refs):
    for k in range(4):
        y_at = lax.rem(place[3] - k + 4, 4)
        row = pl.multiple_of(lax.div(y_at, 2) * GROUP, GROUP)
        lane = pl.multiple_of(lax.rem(y_at, 2) * LANES, LANES)
        for step in range(2):
            refs[4 + step][pl.ds(row, GROUP), pl.ds(lane, LANES)] = refs[k][step]


def run_merge(place, from_y):
    vmem = pl.BlockSpec(memory_space=pltpu.VMEM)
    return pl.pallas_call(
        merge_kernel,
        out_shape=[jax.ShapeDtypeStruct((2 * GROUP, 2 * LANES), jnp.bfloat16)] * 2,
        in_specs=[pl.BlockSpec(memory_space=pltpu.SMEM)] + [vmem] * 4,
        out_specs=[vmem] * 2,
        compiler_params=SMALL,
        name="merge",
    )(place, *from_y)


def handed_kernel(place, lower_ref, *refs):
    copies = [pltpu.make_async_copy(refs[k].at[place[4]], refs[3 + k], refs[6].at[k]) for k in range(3)]
    for copy in copies:
        copy.start()
    for copy in copies:
        copy.wait()


def run_handed(place, lower, panels):
    hbm = pl.BlockSpec(memory_space=pltpu.HBM)
    return pl.pallas_call(
        handed_kernel,
        out_shape=[jax.ShapeDtypeStruct(p.shape[1:], p.dtype) for p in panels],
        in_specs=[pl.BlockSpec(memory_space=pltpu.SMEM), pl.BlockSpec(memory_space=pltpu.VMEM)] + [hbm] * 3,
        out_specs=[hbm] * 3,
        scratch_shapes=[pltpu.SemaphoreType.DMA((3,))],
        compiler_params=SMALL,
        cost_estimate=pl.CostEstimate(flops=0, bytes_accessed=6 * 2**20, transcendentals=0),
        name="handed",
    )(place, lower, *panels)


def swapped_kernel(place, *refs):
    slot = place[4]
    copies = []
    for k in range(3):
        panel, taken, out = refs[k], refs[3 + k], refs[6 + k]
        copies.append(pltpu.make_async_copy(panel.at[1 - slot], out.at[1 - slot], refs[9].at[2 * k]))
        copies.append(pltpu.make_async_copy(taken, out.at[slot], refs[9].at[2 * k + 1]))
    for copy in copies:
        copy.start()
    for copy in copies:
        copy.wait()


def run_swapped(place, panels, taken):
    hbm = pl.BlockSpec(memory_space=pltpu.HBM)
    return pl.pallas_call(
        swapped_kernel,
        out_shape=[jax.ShapeDtypeStruct(p.shape, p.dtype) for p in panels],
        in_specs=[pl.BlockSpec(memory_space=pltpu.SMEM)] + [hbm] * 6,
        out_specs=[hbm] * 3,
        scratch_shapes=[pltpu.SemaphoreType.DMA((6,))],
        compiler_params=SMALL,
        cost_estimate=pl.CostEstimate(flops=0, bytes_accessed=11 * 2**20, transcendentals=0),
        name="swapped",
    )(place, *panels, *taken)


def layer_kernel(z_last, *refs):
    n_pieces = 1 if z_last else 4
    place, position_ref = refs[:2]
    pieces = refs[2 : 2 + n_pieces]
    gate_own, up_own, down_own, gate_other, up_other, down_other = refs[2 + n_pieces : 8 + n_pieces]
    outs = refs[8 + n_pieces : 8 + 2 * n_pieces]
    count_ref = refs[8 + 2 * n_pieces]
    rows_ref, panel_ref, down_ref, result_ref, sems = refs[9 + 2 * n_pieces :]
    my_x, my_core, chip = place[0], place[1], place[2]

    copies = []
    for q, (gate_w, up_w, slot) in enumerate(
        ((gate_own, up_own, 0), (gate_own, up_own, 1), (gate_other, up_other, 0), (gate_other, up_other, 1))
    ):
        copies.append(
            [
                pltpu.make_async_copy(gate_w.at[slot], panel_ref.at[q, :, :WIDTH, :128], sems.at[2 * q]),
                pltpu.make_async_copy(up_w.at[slot], panel_ref.at[q, :, :WIDTH, 128:], sems.at[2 * q + 1]),
            ]
        )
    copies.append([pltpu.make_async_copy(down_own, down_ref.at[:2], sems.at[8])])
    copies.append([pltpu.make_async_copy(down_other, down_ref.at[2:], sems.at[9])])
    for group in copies:
        for copy in group:
            copy.start()

    for q in range(4):
        panel_ref[q, :, WIDTH:, :] = jnp.zeros((8, LANES - WIDTH, 256), jnp.bfloat16)
    for zr in range(8):
        for xr in range(4):
            x_at = lax.rem(my_x - xr + 4, 4)
            lane = pl.multiple_of(x_at * 2 * LANES, 2 * LANES)
            piece = pieces[0].at[zr, xr] if z_last else pieces[xr].at[zr]
            rows_ref[zr * 2 * GROUP : (zr + 1) * 2 * GROUP, pl.ds(lane, 2 * LANES)] = piece[...]

    gates = rows_ref[:, WIDTH:LANES].astype(jnp.float32) * 256.0
    gates = gates + rows_ref[:, LANES + WIDTH : 2 * LANES].astype(jnp.float32)
    count_ref[...] = jnp.broadcast_to(
        jnp.sum((gates > 0.0).astype(jnp.float32), axis=0, keepdims=True), count_ref.shape
    )
    positions = position_ref[...]
    hidden = []
    for q in range(4):
        stored = chip * 4 + (my_core if q < 2 else 1 - my_core) * 2 + q % 2
        share = jnp.sum(jnp.where(positions == stored, gates, 0.0), axis=1, keepdims=True) * (1.0 / 65536.0)
        for copy in copies[q]:
            copy.wait()
        act = jnp.dot(
            rows_ref[...], panel_ref[q].reshape(8 * LANES, 256), preferred_element_type=jnp.float32
        )
        hidden.append((jax.nn.silu(act[:, :128]) * act[:, 128:] * share).astype(jnp.bfloat16))
    hidden = jnp.concatenate(hidden, axis=1)
    for group in copies[4:]:
        for copy in group:
            copy.wait()
    for x_at in range(4):
        panel = down_ref[:, :, x_at * PAIR : (x_at + 1) * PAIR].reshape(4 * 128, PAIR)
        result_ref[x_at] = jnp.dot(hidden, panel, preferred_element_type=jnp.float32).astype(jnp.bfloat16)

    for zr in range(8):
        for xr in range(4):
            x_at = lax.rem(my_x - xr + 4, 4)
            out = outs[0].at[zr, xr] if z_last else outs[xr].at[zr]
            out[...] = result_ref[x_at, zr * 2 * GROUP : (zr + 1) * 2 * GROUP, :]


def run_layer(z_last, place, position, pieces, weights):
    vmem = pl.BlockSpec(memory_space=pltpu.VMEM)
    shape = pieces[0].shape[:-1] + (PAIR,)
    out = pl.pallas_call(
        functools.partial(layer_kernel, z_last),
        out_shape=[jax.ShapeDtypeStruct(shape, jnp.bfloat16)] * len(pieces)
        + [jax.ShapeDtypeStruct((8, 64), jnp.float32)],
        in_specs=[pl.BlockSpec(memory_space=pltpu.SMEM)]
        + [vmem] * (1 + len(pieces))
        + [pl.BlockSpec(memory_space=pltpu.HBM)] * 6,
        out_specs=[vmem] * (len(pieces) + 1),
        scratch_shapes=[
            pltpu.VMEM((256, 8 * LANES), jnp.bfloat16),
            pltpu.VMEM((4, 8, LANES, 256), jnp.bfloat16),
            pltpu.VMEM((4, 128, 3584), jnp.bfloat16),
            pltpu.VMEM((4, 256, PAIR), jnp.bfloat16),
            pltpu.SemaphoreType.DMA((10,)),
        ],
        compiler_params=pltpu.CompilerParams(vmem_limit_bytes=52 * 2**20),
        cost_estimate=pl.CostEstimate(flops=2 * 256 * 3584 * 1536, bytes_accessed=16 * 2**20, transcendentals=0),
        name="layer_z_last" if z_last else "layer_x_last",
    )(place, position, *pieces, *weights)
    return out[:-1], out[-1]


def after(value, *earlier):
    return lax.optimization_barrier((value, earlier))[0]


def on_device(tokens, routes, gate_fix, position, swap_slot, w_gate, w_up, w_down):
    yh, z, core = (lax.axis_index(a) for a in EXPERT_AXES)
    x, yl = (lax.axis_index(a) for a in DP_AXES)
    own_index = (yh * 8 + z) * 2 + core
    my_y = yh * 2 + yl
    given_slot = lax.dynamic_index_in_dim(swap_slot, own_index, 0, keepdims=False)
    place = jnp.stack([x, core, yh * 8 + z, my_y, given_slot]).astype(jnp.int32)

    lower = run_ride(place, tokens, routes, gate_fix)
    step_rows = run_merge(place, gather_ring(lower, Y))

    swap_core, swap_y = [(0, 1), (1, 0)], [(0, 1), (1, 0)]
    panels = (w_gate.reshape(2, 8, WIDTH, 128), w_up.reshape(2, 8, WIDTH, 128), w_down)
    other = tuple(lax.ppermute(w, "core", swap_core) for w in panels)
    weights = panels + other
    gate_given, up_given, down_given = run_handed(place, lower, panels)
    gate_taken = lax.ppermute(after(gate_given, *step_rows), "yh", swap_y)
    up_taken = lax.ppermute(after(up_given, gate_taken), "yh", swap_y)
    down_taken = lax.ppermute(after(down_given, up_taken), "yh", swap_y)

    piece0 = lax.all_gather(jnp.stack(gather_ring(step_rows[0], "x")), "z")
    pieces1 = gather_ring(gather_z(after(step_rows[1], *other)), "x")
    positions = position.reshape(1, 64)
    out1, counts = run_layer(False, after(place, gate_taken), positions, pieces1, weights)
    out0, _ = run_layer(True, after(place, up_taken, counts), positions, [piece0], weights)

    back0 = lax.psum_scatter(out0[0], "z", scatter_dimension=0)
    back0 = after(back0, down_taken)
    back1 = reduce_ring(out1, "x")
    back1 = reduce_z(back1)
    back0 = reduce_ring([back0[k] for k in range(4)], "x")
    back = jnp.stack([back0, back1]).reshape(2, 2, GROUP, PAIR)
    halves = [back[:, 0, :, :WIDTH], back[:, 0, :, WIDTH:], back[:, 1, :, :WIDTH], back[:, 1, :, WIDTH:]]
    combined = reduce_ring([lax.select_n(lax.rem(my_y - k + 4, 4), *halves) for k in range(4)], Y)

    counts = counts[0] + lax.ppermute(counts[0], "core", swap_core)
    holder, held_slot = position // 2, position % 2
    partner = jnp.bitwise_xor(holder, 16)
    owners = jnp.arange(32, dtype=jnp.int32)
    slot_of = lambda h: jnp.sum(jnp.where(h[:, None] == owners, swap_slot, 0), axis=1)
    new_holder = jnp.where(held_slot == slot_of(holder), partner, holder)
    device_load = (jnp.sum(jnp.where(new_holder == own_index, counts, 0.0)) / 128.0).reshape(1)

    new = run_swapped(place, panels, (gate_taken, up_taken, down_taken))
    return (combined, device_load, *[n.reshape(w.shape) for n, w in zip(new, (w_gate, w_up, w_down))])


def solution(mesh):
    fine = Mesh(mesh.devices.reshape(tuple(SIZES.values())), tuple(SIZES))
    in_specs = (
        P(None, EXPERT_AXES, DP_AXES),
        P(None, EXPERT_AXES, None),
        P(None, EXPERT_AXES, None),
        P(),
        P(),
        P(EXPERT_AXES, None, DP_AXES),
        P(EXPERT_AXES, None, DP_AXES),
        P(EXPERT_AXES, DP_AXES, None),
    )
    out_specs = (
        P(None, EXPERT_AXES, DP_AXES),
        P(EXPERT_AXES),
        P(EXPERT_AXES, None, DP_AXES),
        P(EXPERT_AXES, None, DP_AXES),
        P(EXPERT_AXES, DP_AXES, None),
    )
    return jax.shard_map(on_device, mesh=fine, in_specs=in_specs, out_specs=out_specs, check_vma=False)
```

```python
import functools

import jax
import jax.numpy as jnp
import numpy as np
from jax import lax
from jax.experimental import pallas as pl
from jax.experimental.pallas import tpu as pltpu
from jax.sharding import Mesh, PartitionSpec as P

SIZES = {"yh": 2, "z": 8, "core": 2, "x": 4, "yl": 2}
EXPERT_AXES = ("yh", "z", "core")
DP_AXES = ("x", "yl")
Y = ("yh", "yl")
GROUP = 16
WIDTH = 448
PAIR = 2 * WIDTH
LANES = 512
LARGE = pltpu.CompilerParams(vmem_limit_bytes=60 * 2**20)
SMALL = pltpu.CompilerParams(vmem_limit_bytes=4 * 2**20)


def ring_size(axes):
    return int(np.prod([SIZES[a] for a in axes]))


def send(value, axes, amount):
    count = ring_size(axes)
    return lax.ppermute(value, axes, [(i, (i + amount) % count) for i in range(count)])


def total(values):
    return functools.reduce(jnp.add, [v.astype(jnp.float32) for v in values]).astype(jnp.bfloat16)


def gather_ring(value, axes):
    return [value] + [send(value, axes, k) for k in range(1, ring_size(axes))]


def reduce_ring(pieces, axes):
    return total([pieces[0]] + [send(piece, axes, -k) for k, piece in enumerate(pieces) if k])


def gather_z(value):
    back, ahead, far = send(value, "z", 1), send(value, "z", -1), send(value, "z", 4)
    back2 = send(jnp.stack([value, back]), "z", 2)
    ahead2 = send(jnp.stack([value, ahead]), "z", -2)
    return run_join([value[None], back[None], back2, far[None], ahead2, ahead[None]])


def run_join(parts):
    vmem = pl.BlockSpec(memory_space=pltpu.VMEM)

    def join_kernel(*refs):
        at = 0
        for ref in refs[:-1]:
            refs[-1][at : at + ref.shape[0]] = ref[...]
            at += ref.shape[0]

    count = sum(p.shape[0] for p in parts)
    return pl.pallas_call(
        join_kernel,
        out_shape=jax.ShapeDtypeStruct((count,) + parts[0].shape[1:], parts[0].dtype),
        in_specs=[vmem] * len(parts),
        out_specs=vmem,
        compiler_params=SMALL,
        name="join",
    )(*parts)


def reduce_z(pieces):
    back2 = send(pieces[2:4], "z", -2)
    ahead2 = send(pieces[5:7], "z", 2)
    far = send(pieces[4], "z", -4)
    back = send(total([pieces[1], back2[1]]), "z", -1)
    ahead = send(total([pieces[7], ahead2[1]]), "z", 1)
    return total([pieces[0], back2[0], ahead2[0], far, back, ahead])


def ride_kernel(place, tokens_ref, routes_ref, gate_ref, out_ref):
    labels = lax.broadcasted_iota(jnp.int32, (2, GROUP, LANES - WIDTH), 2)
    gate = gate_ref[...]
    part = jnp.where(lax.rem(place[3], 2) == 0, gate >> 8, gate & 255)
    routes = routes_ref[...]
    ride = jnp.zeros(labels.shape, jnp.int32)
    for k in range(routes.shape[2]):
        ride = ride + jnp.where(routes[:, :, k : k + 1] == labels, part[:, :, k : k + 1], 0)
    ride = ride.astype(jnp.float32).astype(jnp.bfloat16)
    out_ref[...] = jnp.concatenate([tokens_ref[...], ride], axis=2)


def run_ride(place, tokens, routes, gate_fix):
    vmem = pl.BlockSpec(memory_space=pltpu.VMEM)
    return pl.pallas_call(
        ride_kernel,
        out_shape=jax.ShapeDtypeStruct((2, GROUP, LANES), jnp.bfloat16),
        in_specs=[pl.BlockSpec(memory_space=pltpu.SMEM)] + [vmem] * 3,
        out_specs=vmem,
        compiler_params=SMALL,
        name="ride",
    )(place, tokens, routes, gate_fix)


def merge_kernel(place, *refs):
    for k in range(4):
        y_at = lax.rem(place[3] - k + 4, 4)
        row = pl.multiple_of(lax.div(y_at, 2) * GROUP, GROUP)
        lane = pl.multiple_of(lax.rem(y_at, 2) * LANES, LANES)
        for step in range(2):
            refs[4 + step][pl.ds(row, GROUP), pl.ds(lane, LANES)] = refs[k][step]


def run_merge(place, from_y):
    vmem = pl.BlockSpec(memory_space=pltpu.VMEM)
    return pl.pallas_call(
        merge_kernel,
        out_shape=[jax.ShapeDtypeStruct((2 * GROUP, 2 * LANES), jnp.bfloat16)] * 2,
        in_specs=[pl.BlockSpec(memory_space=pltpu.SMEM)] + [vmem] * 4,
        out_specs=[vmem] * 2,
        compiler_params=SMALL,
        name="merge",
    )(place, *from_y)


def handed_kernel(place, lower_ref, *refs):
    copies = [pltpu.make_async_copy(refs[k].at[place[4]], refs[3 + k], refs[6].at[k]) for k in range(3)]
    for copy in copies:
        copy.start()
    for copy in copies:
        copy.wait()


def run_handed(place, lower, panels):
    hbm = pl.BlockSpec(memory_space=pltpu.HBM)
    return pl.pallas_call(
        handed_kernel,
        out_shape=[jax.ShapeDtypeStruct(p.shape[1:], p.dtype) for p in panels],
        in_specs=[pl.BlockSpec(memory_space=pltpu.SMEM), pl.BlockSpec(memory_space=pltpu.VMEM)] + [hbm] * 3,
        out_specs=[hbm] * 3,
        scratch_shapes=[pltpu.SemaphoreType.DMA((3,))],
        compiler_params=LARGE,
        cost_estimate=pl.CostEstimate(flops=0, bytes_accessed=6 * 2**20, transcendentals=0),
        name="handed",
    )(place, lower, *panels)


def swapped_kernel(place, *refs):
    slot = place[4]
    copies = []
    for k in range(3):
        panel, taken, out = refs[k], refs[3 + k], refs[6 + k]
        copies.append(pltpu.make_async_copy(panel.at[1 - slot], out.at[1 - slot], refs[9].at[2 * k]))
        copies.append(pltpu.make_async_copy(taken, out.at[slot], refs[9].at[2 * k + 1]))
    for copy in copies:
        copy.start()
    for copy in copies:
        copy.wait()


def run_swapped(place, panels, taken):
    hbm = pl.BlockSpec(memory_space=pltpu.HBM)
    return pl.pallas_call(
        swapped_kernel,
        out_shape=[jax.ShapeDtypeStruct(p.shape, p.dtype) for p in panels],
        in_specs=[pl.BlockSpec(memory_space=pltpu.SMEM)] + [hbm] * 6,
        out_specs=[hbm] * 3,
        scratch_shapes=[pltpu.SemaphoreType.DMA((6,))],
        compiler_params=LARGE,
        cost_estimate=pl.CostEstimate(flops=0, bytes_accessed=11 * 2**20, transcendentals=0),
        name="swapped",
    )(place, *panels, *taken)


def layer_kernel(place, position_ref, *refs):
    piece0, pieces1 = refs[0], refs[1:5]
    gate_own, up_own, down_own, gate_other, up_other, down_other = refs[5:11]
    out0, outs1, count_ref = refs[11], refs[12:16], refs[16]
    rows_ref, panel_ref, down_ref, result_ref, sems = refs[17:]
    my_x, my_core, chip = place[0], place[1], place[2]
    span = 2 * GROUP

    copies = []
    for q, (gate_w, up_w, slot) in enumerate(
        ((gate_own, up_own, 0), (gate_own, up_own, 1), (gate_other, up_other, 0), (gate_other, up_other, 1))
    ):
        copies.append(
            [
                pltpu.make_async_copy(gate_w.at[slot], panel_ref.at[q, :, :WIDTH, :128], sems.at[2 * q]),
                pltpu.make_async_copy(up_w.at[slot], panel_ref.at[q, :, :WIDTH, 128:], sems.at[2 * q + 1]),
            ]
        )
    copies.append([pltpu.make_async_copy(down_own, down_ref.at[:2], sems.at[8])])
    copies.append([pltpu.make_async_copy(down_other, down_ref.at[2:], sems.at[9])])
    for group in copies:
        for copy in group:
            copy.start()

    for q in range(4):
        panel_ref[q, :, WIDTH:, :] = jnp.zeros((8, LANES - WIDTH, 256), jnp.bfloat16)
    for xr in range(4):
        x_at = lax.rem(my_x - xr + 4, 4)
        lanes = pl.ds(pl.multiple_of(x_at * 2 * LANES, 2 * LANES), 2 * LANES)
        for zr in range(8):
            rows_ref[zr * span : (zr + 1) * span, lanes] = piece0[zr, xr]
            rows_ref[(8 + zr) * span : (9 + zr) * span, lanes] = pieces1[xr][zr]

    gates = rows_ref[:, WIDTH:LANES].astype(jnp.float32) * 256.0
    gates = gates + rows_ref[:, LANES + WIDTH : 2 * LANES].astype(jnp.float32)
    count_ref[...] = jnp.broadcast_to(
        jnp.sum((gates[8 * span :] > 0.0).astype(jnp.float32), axis=0, keepdims=True), count_ref.shape
    )
    positions = position_ref[...]
    hidden = []
    for q in range(4):
        stored = chip * 4 + (my_core if q < 2 else 1 - my_core) * 2 + q % 2
        share = jnp.sum(jnp.where(positions == stored, gates, 0.0), axis=1, keepdims=True) * (1.0 / 65536.0)
        for copy in copies[q]:
            copy.wait()
        act = jnp.dot(
            rows_ref[...], panel_ref[q].reshape(8 * LANES, 256), preferred_element_type=jnp.float32
        )
        hidden.append((jax.nn.silu(act[:, :128]) * act[:, 128:] * share).astype(jnp.bfloat16))
    hidden = jnp.concatenate(hidden, axis=1)
    for group in copies[4:]:
        for copy in group:
            copy.wait()
    for x_at in range(4):
        panel = down_ref[:, :, x_at * PAIR : (x_at + 1) * PAIR].reshape(4 * 128, PAIR)
        result_ref[x_at] = jnp.dot(hidden, panel, preferred_element_type=jnp.float32).astype(jnp.bfloat16)

    for xr in range(4):
        x_at = lax.rem(my_x - xr + 4, 4)
        for zr in range(8):
            out0[zr, xr] = result_ref[x_at, zr * span : (zr + 1) * span, :]
            outs1[xr][zr] = result_ref[x_at, (8 + zr) * span : (9 + zr) * span, :]


def run_layer(place, position, piece0, pieces1, weights):
    vmem = pl.BlockSpec(memory_space=pltpu.VMEM)
    out = pl.pallas_call(
        layer_kernel,
        out_shape=[jax.ShapeDtypeStruct((8, 4, 2 * GROUP, PAIR), jnp.bfloat16)]
        + [jax.ShapeDtypeStruct((8, 2 * GROUP, PAIR), jnp.bfloat16)] * 4
        + [jax.ShapeDtypeStruct((8, 64), jnp.float32)],
        in_specs=[pl.BlockSpec(memory_space=pltpu.SMEM)]
        + [vmem] * 6
        + [pl.BlockSpec(memory_space=pltpu.HBM)] * 6,
        out_specs=[vmem] * 6,
        scratch_shapes=[
            pltpu.VMEM((512, 8 * LANES), jnp.bfloat16),
            pltpu.VMEM((4, 8, LANES, 256), jnp.bfloat16),
            pltpu.VMEM((4, 128, 3584), jnp.bfloat16),
            pltpu.VMEM((4, 512, PAIR), jnp.bfloat16),
            pltpu.SemaphoreType.DMA((10,)),
        ],
        compiler_params=pltpu.CompilerParams(vmem_limit_bytes=52 * 2**20),
        cost_estimate=pl.CostEstimate(flops=2 * 512 * 3584 * 1536, bytes_accessed=20 * 2**20, transcendentals=0),
        name="layer",
    )(place, position, piece0, *pieces1, *weights)
    return out[0], out[1:5], out[5]


def after(value, *earlier):
    return lax.optimization_barrier((value, earlier))[0]


def on_device(tokens, routes, gate_fix, position, swap_slot, w_gate, w_up, w_down):
    yh, z, core = (lax.axis_index(a) for a in EXPERT_AXES)
    x, yl = (lax.axis_index(a) for a in DP_AXES)
    own_index = (yh * 8 + z) * 2 + core
    my_y = yh * 2 + yl
    given_slot = lax.dynamic_index_in_dim(swap_slot, own_index, 0, keepdims=False)
    place = jnp.stack([x, core, yh * 8 + z, my_y, given_slot]).astype(jnp.int32)

    lower = run_ride(place, tokens, routes, gate_fix)
    step_rows = run_merge(place, gather_ring(lower, Y))

    swap_core, swap_y = [(0, 1), (1, 0)], [(0, 1), (1, 0)]
    panels = (w_gate.reshape(2, 8, WIDTH, 128), w_up.reshape(2, 8, WIDTH, 128), w_down)
    other = tuple(lax.ppermute(w, "core", swap_core) for w in panels)
    weights = panels + other
    gate_given, up_given, down_given = run_handed(place, lower, panels)
    gate_taken = lax.ppermute(after(gate_given, *step_rows), "yh", swap_y)
    piece0 = lax.all_gather(jnp.stack(gather_ring(step_rows[0], "x")), "z")
    over_z = gather_z(after(step_rows[1], *other))
    up_taken = lax.ppermute(after(up_given, gate_taken, over_z), "yh", swap_y)
    down_taken = lax.ppermute(after(down_given, up_taken), "yh", swap_y)
    pieces1 = gather_ring(over_z, "x")
    out0, out1, counts = run_layer(after(place, up_taken), position.reshape(1, 64), piece0, pieces1, weights)
    new = run_swapped(place, panels, (gate_taken, up_taken, down_taken))

    back0 = lax.psum_scatter(out0, "z", scatter_dimension=0)
    back0 = after(back0, *new)
    back1 = reduce_ring(out1, "x")
    back1 = reduce_z(back1)
    back0 = reduce_ring([back0[k] for k in range(4)], "x")
    back = jnp.stack([back0, back1]).reshape(2, 2, GROUP, PAIR)
    halves = [back[:, 0, :, :WIDTH], back[:, 0, :, WIDTH:], back[:, 1, :, :WIDTH], back[:, 1, :, WIDTH:]]
    combined = reduce_ring([lax.select_n(lax.rem(my_y - k + 4, 4), *halves) for k in range(4)], Y)

    counts = counts[0] + lax.ppermute(counts[0], "core", swap_core)
    holder, held_slot = position // 2, position % 2
    partner = jnp.bitwise_xor(holder, 16)
    owners = jnp.arange(32, dtype=jnp.int32)
    slot_of = lambda h: jnp.sum(jnp.where(h[:, None] == owners, swap_slot, 0), axis=1)
    new_holder = jnp.where(held_slot == slot_of(holder), partner, holder)
    device_load = (jnp.sum(jnp.where(new_holder == own_index, counts, 0.0)) / 128.0).reshape(1)

    return (combined, device_load, *[n.reshape(w.shape) for n, w in zip(new, (w_gate, w_up, w_down))])


def solution(mesh):
    fine = Mesh(mesh.devices.reshape(tuple(SIZES.values())), tuple(SIZES))
    in_specs = (
        P(None, EXPERT_AXES, DP_AXES),
        P(None, EXPERT_AXES, None),
        P(None, EXPERT_AXES, None),
        P(),
        P(),
        P(EXPERT_AXES, None, DP_AXES),
        P(EXPERT_AXES, None, DP_AXES),
        P(EXPERT_AXES, DP_AXES, None),
    )
    out_specs = (
        P(None, EXPERT_AXES, DP_AXES),
        P(EXPERT_AXES),
        P(EXPERT_AXES, None, DP_AXES),
        P(EXPERT_AXES, None, DP_AXES),
        P(EXPERT_AXES, DP_AXES, None),
    )
    return jax.shard_map(on_device, mesh=fine, in_specs=in_specs, out_specs=out_specs, check_vma=False)
```

```python
import functools

import jax
import jax.numpy as jnp
import numpy as np
from jax import lax
from jax.experimental import pallas as pl
from jax.experimental.pallas import tpu as pltpu
from jax.sharding import Mesh, PartitionSpec as P

SIZES = {"yh": 2, "z": 8, "core": 2, "x": 4, "yl": 2}
EXPERT_AXES = ("yh", "z", "core")
DP_AXES = ("x", "yl")
Y = ("yh", "yl")
GROUP = 16
WIDTH = 448
PAIR = 2 * WIDTH
LANES = 512
LARGE = pltpu.CompilerParams(vmem_limit_bytes=60 * 2**20)
SMALL = pltpu.CompilerParams(vmem_limit_bytes=4 * 2**20)


def ring_size(axes):
    return int(np.prod([SIZES[a] for a in axes]))


def send(value, axes, amount):
    count = ring_size(axes)
    return lax.ppermute(value, axes, [(i, (i + amount) % count) for i in range(count)])


def total(values):
    return functools.reduce(jnp.add, [v.astype(jnp.float32) for v in values]).astype(jnp.bfloat16)


def gather_ring(value, axes):
    return [value] + [send(value, axes, k) for k in range(1, ring_size(axes))]


def reduce_ring(pieces, axes):
    return total([pieces[0]] + [send(piece, axes, -k) for k, piece in enumerate(pieces) if k])


def gather_z(value):
    back, ahead, far = send(value, "z", 1), send(value, "z", -1), send(value, "z", 4)
    back2 = send(jnp.stack([value, back]), "z", 2)
    ahead2 = send(jnp.stack([value, ahead]), "z", -2)
    return run_join([value[None], back[None], back2, far[None], ahead2, ahead[None]])


def run_join(parts):
    vmem = pl.BlockSpec(memory_space=pltpu.VMEM)

    def join_kernel(*refs):
        at = 0
        for ref in refs[:-1]:
            refs[-1][at : at + ref.shape[0]] = ref[...]
            at += ref.shape[0]

    count = sum(p.shape[0] for p in parts)
    return pl.pallas_call(
        join_kernel,
        out_shape=jax.ShapeDtypeStruct((count,) + parts[0].shape[1:], parts[0].dtype),
        in_specs=[vmem] * len(parts),
        out_specs=vmem,
        compiler_params=SMALL,
        name="join",
    )(*parts)


def reduce_z(pieces):
    back2 = send(pieces[2:4], "z", -2)
    ahead2 = send(pieces[5:7], "z", 2)
    far = send(pieces[4], "z", -4)
    back = send(total([pieces[1], back2[1]]), "z", -1)
    ahead = send(total([pieces[7], ahead2[1]]), "z", 1)
    return total([pieces[0], back2[0], ahead2[0], far, back, ahead])


def ride_kernel(place, tokens_ref, routes_ref, gate_ref, out_ref):
    labels = lax.broadcasted_iota(jnp.int32, (2, GROUP, LANES - WIDTH), 2)
    gate = gate_ref[...]
    part = jnp.where(lax.rem(place[3], 2) == 0, gate >> 8, gate & 255)
    routes = routes_ref[...]
    ride = jnp.zeros(labels.shape, jnp.int32)
    for k in range(routes.shape[2]):
        ride = ride + jnp.where(routes[:, :, k : k + 1] == labels, part[:, :, k : k + 1], 0)
    ride = ride.astype(jnp.float32).astype(jnp.bfloat16)
    out_ref[...] = jnp.concatenate([tokens_ref[...], ride], axis=2)


def run_ride(place, tokens, routes, gate_fix):
    vmem = pl.BlockSpec(memory_space=pltpu.VMEM)
    return pl.pallas_call(
        ride_kernel,
        out_shape=jax.ShapeDtypeStruct((2, GROUP, LANES), jnp.bfloat16),
        in_specs=[pl.BlockSpec(memory_space=pltpu.SMEM)] + [vmem] * 3,
        out_specs=vmem,
        compiler_params=SMALL,
        name="ride",
    )(place, tokens, routes, gate_fix)


def merge_kernel(place, *refs):
    for k in range(4):
        y_at = lax.rem(place[3] - k + 4, 4)
        row = pl.multiple_of(lax.div(y_at, 2) * GROUP, GROUP)
        lane = pl.multiple_of(lax.rem(y_at, 2) * LANES, LANES)
        for step in range(2):
            refs[4 + step][pl.ds(row, GROUP), pl.ds(lane, LANES)] = refs[k][step]


def run_merge(place, from_y):
    vmem = pl.BlockSpec(memory_space=pltpu.VMEM)
    return pl.pallas_call(
        merge_kernel,
        out_shape=[jax.ShapeDtypeStruct((2 * GROUP, 2 * LANES), jnp.bfloat16)] * 2,
        in_specs=[pl.BlockSpec(memory_space=pltpu.SMEM)] + [vmem] * 4,
        out_specs=[vmem] * 2,
        compiler_params=SMALL,
        name="merge",
    )(place, *from_y)


def handed_kernel(place, lower_ref, *refs):
    ins = [pltpu.make_async_copy(refs[k].at[place[4]], refs[6 + k], refs[9].at[k]) for k in range(3)]
    outs = [pltpu.make_async_copy(refs[6 + k], refs[3 + k], refs[9].at[3 + k]) for k in range(3)]
    for copy in ins:
        copy.start()
    for copy_in, copy_out in zip(ins, outs):
        copy_in.wait()
        copy_out.start()
    for copy in outs:
        copy.wait()


def run_handed(place, lower, panels):
    hbm = pl.BlockSpec(memory_space=pltpu.HBM)
    return pl.pallas_call(
        handed_kernel,
        out_shape=[jax.ShapeDtypeStruct(p.shape[1:], p.dtype) for p in panels],
        in_specs=[pl.BlockSpec(memory_space=pltpu.SMEM), pl.BlockSpec(memory_space=pltpu.VMEM)] + [hbm] * 3,
        out_specs=[hbm] * 3,
        scratch_shapes=[pltpu.VMEM(p.shape[1:], p.dtype) for p in panels] + [pltpu.SemaphoreType.DMA((6,))],
        compiler_params=LARGE,
        cost_estimate=pl.CostEstimate(flops=0, bytes_accessed=6 * 2**20, transcendentals=0),
        name="handed",
    )(place, lower, *panels)


def swapped_kernel(place, *refs):
    slot = place[4]
    ins, outs = [], []
    for k in range(3):
        panel, taken, out, room = refs[k], refs[3 + k], refs[6 + k], refs[9 + k]
        for j, source, at in ((0, panel.at[1 - slot], 1 - slot), (1, taken, slot)):
            ins.append(pltpu.make_async_copy(source, room.at[j], refs[12].at[2 * k + j]))
            outs.append(pltpu.make_async_copy(room.at[j], out.at[at], refs[12].at[6 + 2 * k + j]))
    for copy in ins:
        copy.start()
    for copy_in, copy_out in zip(ins, outs):
        copy_in.wait()
        copy_out.start()
    for copy in outs:
        copy.wait()


def run_swapped(place, panels, taken):
    hbm = pl.BlockSpec(memory_space=pltpu.HBM)
    return pl.pallas_call(
        swapped_kernel,
        out_shape=[jax.ShapeDtypeStruct(p.shape, p.dtype) for p in panels],
        in_specs=[pl.BlockSpec(memory_space=pltpu.SMEM)] + [hbm] * 6,
        out_specs=[hbm] * 3,
        scratch_shapes=[pltpu.VMEM(p.shape, p.dtype) for p in panels] + [pltpu.SemaphoreType.DMA((12,))],
        compiler_params=LARGE,
        cost_estimate=pl.CostEstimate(flops=0, bytes_accessed=11 * 2**20, transcendentals=0),
        name="swapped",
    )(place, *panels, *taken)


def layer_kernel(place, position_ref, *refs):
    piece0, pieces1 = refs[0], refs[1:5]
    gate_own, up_own, down_own, gate_other, up_other, down_other = refs[5:11]
    out0, outs1, count_ref = refs[11], refs[12:16], refs[16]
    rows_ref, panel_ref, down_ref, hidden_ref, result_ref, sems = refs[17:]
    my_x, my_core, chip = place[0], place[1], place[2]
    span = 2 * GROUP

    copies = []
    for q, (gate_w, up_w, slot) in enumerate(
        ((gate_own, up_own, 0), (gate_own, up_own, 1), (gate_other, up_other, 0), (gate_other, up_other, 1))
    ):
        copies.append(
            [
                pltpu.make_async_copy(gate_w.at[slot], panel_ref.at[q, :, :WIDTH, :128], sems.at[2 * q]),
                pltpu.make_async_copy(up_w.at[slot], panel_ref.at[q, :, :WIDTH, 128:], sems.at[2 * q + 1]),
            ]
        )
    copies.append([pltpu.make_async_copy(down_own, down_ref.at[:2], sems.at[8])])
    copies.append([pltpu.make_async_copy(down_other, down_ref.at[2:], sems.at[9])])
    for group in copies:
        for copy in group:
            copy.start()

    for q in range(4):
        panel_ref[q, :, WIDTH:, :] = jnp.zeros((8, LANES - WIDTH, 256), jnp.bfloat16)
    for xr in range(4):
        x_at = lax.rem(my_x - xr + 4, 4)
        lanes = pl.ds(pl.multiple_of(x_at * 2 * LANES, 2 * LANES), 2 * LANES)
        for zr in range(8):
            rows_ref[zr * span : (zr + 1) * span, lanes] = piece0[zr, xr]
            rows_ref[(8 + zr) * span : (9 + zr) * span, lanes] = pieces1[xr][zr]

    gates = rows_ref[:, WIDTH:LANES].astype(jnp.float32) * 256.0
    gates = gates + rows_ref[:, LANES + WIDTH : 2 * LANES].astype(jnp.float32)
    count_ref[...] = jnp.broadcast_to(
        jnp.sum((gates[8 * span :] > 0.0).astype(jnp.float32), axis=0, keepdims=True), count_ref.shape
    )
    positions = position_ref[...]
    for q in range(4):
        stored = chip * 4 + (my_core if q < 2 else 1 - my_core) * 2 + q % 2
        share = jnp.sum(jnp.where(positions == stored, gates, 0.0), axis=1, keepdims=True) * (1.0 / 65536.0)
        for copy in copies[q]:
            copy.wait()
        for step in range(2):
            at = slice(step * 256, (step + 1) * 256)
            act = jnp.zeros((256, 256), jnp.float32)
            for block in range(8):
                act = act + jnp.dot(
                    rows_ref[at, block * LANES : (block + 1) * LANES],
                    panel_ref[q, block],
                    preferred_element_type=jnp.float32,
                )
            value = jax.nn.silu(act[:, :128]) * act[:, 128:] * share[at]
            hidden_ref[at, q * 128 : (q + 1) * 128] = value.astype(jnp.bfloat16)
    for group in copies[4:]:
        for copy in group:
            copy.wait()
    for x_at in range(4):
        panel = down_ref[:, :, x_at * PAIR : (x_at + 1) * PAIR].reshape(4 * 128, PAIR)
        result_ref[x_at] = jnp.dot(hidden_ref[...], panel, preferred_element_type=jnp.float32).astype(jnp.bfloat16)

    for xr in range(4):
        x_at = lax.rem(my_x - xr + 4, 4)
        for zr in range(8):
            out0[zr, xr] = result_ref[x_at, zr * span : (zr + 1) * span, :]
            outs1[xr][zr] = result_ref[x_at, (8 + zr) * span : (9 + zr) * span, :]


def run_layer(place, position, piece0, pieces1, weights):
    vmem = pl.BlockSpec(memory_space=pltpu.VMEM)
    out = pl.pallas_call(
        layer_kernel,
        out_shape=[jax.ShapeDtypeStruct((8, 4, 2 * GROUP, PAIR), jnp.bfloat16)]
        + [jax.ShapeDtypeStruct((8, 2 * GROUP, PAIR), jnp.bfloat16)] * 4
        + [jax.ShapeDtypeStruct((8, 64), jnp.float32)],
        in_specs=[pl.BlockSpec(memory_space=pltpu.SMEM)]
        + [vmem] * 6
        + [pl.BlockSpec(memory_space=pltpu.HBM)] * 6,
        out_specs=[vmem] * 6,
        scratch_shapes=[
            pltpu.VMEM((512, 8 * LANES), jnp.bfloat16),
            pltpu.VMEM((4, 8, LANES, 256), jnp.bfloat16),
            pltpu.VMEM((4, 128, 3584), jnp.bfloat16),
            pltpu.VMEM((512, 512), jnp.bfloat16),
            pltpu.VMEM((4, 512, PAIR), jnp.bfloat16),
            pltpu.SemaphoreType.DMA((10,)),
        ],
        compiler_params=pltpu.CompilerParams(vmem_limit_bytes=52 * 2**20),
        cost_estimate=pl.CostEstimate(flops=2 * 512 * 3584 * 1536, bytes_accessed=20 * 2**20, transcendentals=0),
        name="layer",
    )(place, position, piece0, *pieces1, *weights)
    return out[0], out[1:5], out[5]


def after(value, *earlier):
    return lax.optimization_barrier((value, earlier))[0]


def on_device(tokens, routes, gate_fix, position, swap_slot, w_gate, w_up, w_down):
    yh, z, core = (lax.axis_index(a) for a in EXPERT_AXES)
    x, yl = (lax.axis_index(a) for a in DP_AXES)
    own_index = (yh * 8 + z) * 2 + core
    my_y = yh * 2 + yl
    given_slot = lax.dynamic_index_in_dim(swap_slot, own_index, 0, keepdims=False)
    place = jnp.stack([x, core, yh * 8 + z, my_y, given_slot]).astype(jnp.int32)

    lower = run_ride(place, tokens, routes, gate_fix)
    step_rows = run_merge(place, gather_ring(lower, Y))

    swap_core, swap_y = [(0, 1), (1, 0)], [(0, 1), (1, 0)]
    panels = (w_gate.reshape(2, 8, WIDTH, 128), w_up.reshape(2, 8, WIDTH, 128), w_down)
    other = tuple(lax.ppermute(w, "core", swap_core) for w in panels)
    weights = panels + other
    gate_given, up_given, down_given = run_handed(place, lower, panels)
    gate_taken = lax.ppermute(after(gate_given, *step_rows), "yh", swap_y)
    piece0 = lax.all_gather(jnp.stack(gather_ring(step_rows[0], "x")), "z")
    over_z = gather_z(after(step_rows[1], *other))
    up_taken = lax.ppermute(after(up_given, gate_taken, over_z), "yh", swap_y)
    down_taken = lax.ppermute(after(down_given, up_taken), "yh", swap_y)
    pieces1 = gather_ring(over_z, "x")
    out0, out1, counts = run_layer(after(place, up_taken), position.reshape(1, 64), piece0, pieces1, weights)
    new = run_swapped(place, panels, (gate_taken, up_taken, down_taken))

    back0 = lax.psum_scatter(out0, "z", scatter_dimension=0)
    back0 = after(back0, *new)
    back1 = reduce_ring(out1, "x")
    back1 = reduce_z(back1)
    back0 = reduce_ring([back0[k] for k in range(4)], "x")
    back = jnp.stack([back0, back1]).reshape(2, 2, GROUP, PAIR)
    halves = [back[:, 0, :, :WIDTH], back[:, 0, :, WIDTH:], back[:, 1, :, :WIDTH], back[:, 1, :, WIDTH:]]
    combined = reduce_ring([lax.select_n(lax.rem(my_y - k + 4, 4), *halves) for k in range(4)], Y)

    counts = counts[0] + lax.ppermute(counts[0], "core", swap_core)
    holder, held_slot = position // 2, position % 2
    partner = jnp.bitwise_xor(holder, 16)
    owners = jnp.arange(32, dtype=jnp.int32)
    slot_of = lambda h: jnp.sum(jnp.where(h[:, None] == owners, swap_slot, 0), axis=1)
    new_holder = jnp.where(held_slot == slot_of(holder), partner, holder)
    device_load = (jnp.sum(jnp.where(new_holder == own_index, counts, 0.0)) / 128.0).reshape(1)

    return (combined, device_load, *[n.reshape(w.shape) for n, w in zip(new, (w_gate, w_up, w_down))])


def solution(mesh):
    fine = Mesh(mesh.devices.reshape(tuple(SIZES.values())), tuple(SIZES))
    in_specs = (
        P(None, EXPERT_AXES, DP_AXES),
        P(None, EXPERT_AXES, None),
        P(None, EXPERT_AXES, None),
        P(),
        P(),
        P(EXPERT_AXES, None, DP_AXES),
        P(EXPERT_AXES, None, DP_AXES),
        P(EXPERT_AXES, DP_AXES, None),
    )
    out_specs = (
        P(None, EXPERT_AXES, DP_AXES),
        P(EXPERT_AXES),
        P(EXPERT_AXES, None, DP_AXES),
        P(EXPERT_AXES, None, DP_AXES),
        P(EXPERT_AXES, DP_AXES, None),
    )
    return jax.shard_map(on_device, mesh=fine, in_specs=in_specs, out_specs=out_specs, check_vma=False)
```

```python
import functools

import jax
import jax.numpy as jnp
import numpy as np
from jax import lax
from jax.experimental import pallas as pl
from jax.experimental.pallas import tpu as pltpu
from jax.sharding import Mesh, PartitionSpec as P

SIZES = {"yh": 2, "z": 8, "core": 2, "x": 4, "yl": 2}
EXPERT_AXES = ("yh", "z", "core")
DP_AXES = ("x", "yl")
Y = ("yh", "yl")
GROUP = 16
WIDTH = 448
PAIR = 2 * WIDTH
LANES = 512
LARGE = pltpu.CompilerParams(vmem_limit_bytes=60 * 2**20)
SMALL = pltpu.CompilerParams(vmem_limit_bytes=4 * 2**20)


def ring_size(axes):
    return int(np.prod([SIZES[a] for a in axes]))


def send(value, axes, amount):
    count = ring_size(axes)
    return lax.ppermute(value, axes, [(i, (i + amount) % count) for i in range(count)])


def total(values):
    return functools.reduce(jnp.add, [v.astype(jnp.float32) for v in values]).astype(jnp.bfloat16)


def after(value, *earlier):
    return lax.optimization_barrier((value, earlier))[0]


def gather_ring(value, axes):
    return [value] + [send(value, axes, k) for k in range(1, ring_size(axes))]


def reduce_ring(pieces, axes):
    return total([pieces[0]] + [send(piece, axes, -k) for k, piece in enumerate(pieces) if k])


def gather_z(value, beside):
    first = [send(value, "z", 1), send(value, "z", -1), send(value, "z", 4)]
    back, ahead, far = after(first, *beside)
    back2 = send(jnp.stack([value, back]), "z", 2)
    ahead2 = send(jnp.stack([value, ahead]), "z", -2)
    return run_join([value[None], back[None], back2, far[None], ahead2, ahead[None]])


def run_join(parts):
    vmem = pl.BlockSpec(memory_space=pltpu.VMEM)

    def join_kernel(*refs):
        at = 0
        for ref in refs[:-1]:
            refs[-1][at : at + ref.shape[0]] = ref[...]
            at += ref.shape[0]

    count = sum(p.shape[0] for p in parts)
    return pl.pallas_call(
        join_kernel,
        out_shape=jax.ShapeDtypeStruct((count,) + parts[0].shape[1:], parts[0].dtype),
        in_specs=[vmem] * len(parts),
        out_specs=vmem,
        compiler_params=SMALL,
        name="join",
    )(*parts)


def reduce_z(pieces):
    back2 = send(pieces[2:4], "z", -2)
    ahead2 = send(pieces[5:7], "z", 2)
    far = send(pieces[4], "z", -4)
    back = send(total([pieces[1], back2[1]]), "z", -1)
    ahead = send(total([pieces[7], ahead2[1]]), "z", 1)
    return total([pieces[0], back2[0], ahead2[0], far, back, ahead])


def ride_kernel(place, tokens_ref, routes_ref, gate_ref, out_ref):
    labels = lax.broadcasted_iota(jnp.int32, (LANES - WIDTH, GROUP), 0)
    turn = (
        lax.broadcasted_iota(jnp.int32, (GROUP, GROUP), 0) == lax.broadcasted_iota(jnp.int32, (GROUP, GROUP), 1)
    ).astype(jnp.bfloat16)
    for step in range(2):
        gate, routes = gate_ref[step], routes_ref[step]
        part = jnp.where(lax.rem(place[3], 2) == 0, gate >> 8, gate & 255)
        ride = jnp.zeros(labels.shape, jnp.int32)
        for k in range(routes.shape[0]):
            ride = ride + jnp.where(routes[k : k + 1] == labels, part[k : k + 1], 0)
        ride = ride.astype(jnp.float32).astype(jnp.bfloat16)
        ride = lax.dot_general(turn, ride, (((1,), (1,)), ((), ())), preferred_element_type=jnp.float32)
        out_ref[step] = jnp.concatenate([tokens_ref[step], ride.astype(jnp.bfloat16)], axis=1)


def run_ride(place, tokens, routes, gate_fix):
    vmem = pl.BlockSpec(memory_space=pltpu.VMEM)
    return pl.pallas_call(
        ride_kernel,
        out_shape=jax.ShapeDtypeStruct((2, GROUP, LANES), jnp.bfloat16),
        in_specs=[pl.BlockSpec(memory_space=pltpu.SMEM)] + [vmem] * 3,
        out_specs=vmem,
        compiler_params=SMALL,
        name="ride",
    )(place, tokens, routes.transpose(0, 2, 1), gate_fix.transpose(0, 2, 1))


def merge_kernel(place, *refs):
    for k in range(4):
        y_at = lax.rem(place[3] - k + 4, 4)
        row = pl.multiple_of(lax.div(y_at, 2) * GROUP, GROUP)
        lane = pl.multiple_of(lax.rem(y_at, 2) * LANES, LANES)
        for step in range(2):
            refs[4 + step][pl.ds(row, GROUP), pl.ds(lane, LANES)] = refs[k][step]


def run_merge(place, from_y):
    vmem = pl.BlockSpec(memory_space=pltpu.VMEM)
    return pl.pallas_call(
        merge_kernel,
        out_shape=[jax.ShapeDtypeStruct((2 * GROUP, 2 * LANES), jnp.bfloat16)] * 2,
        in_specs=[pl.BlockSpec(memory_space=pltpu.SMEM)] + [vmem] * 4,
        out_specs=[vmem] * 2,
        compiler_params=SMALL,
        name="merge",
    )(place, *from_y)


def handed_kernel(place, slots, *refs):
    count = (len(refs) - 2) // 3
    slot, sems = slots[place[4]], refs[-1]
    ins = [pltpu.make_async_copy(refs[k].at[slot], refs[2 * count + 1 + k], sems.at[k]) for k in range(count)]
    outs = [pltpu.make_async_copy(refs[2 * count + 1 + k], refs[count + 1 + k], sems.at[count + k]) for k in range(count)]
    for copy in ins:
        copy.start()
    for copy_in, copy_out in zip(ins, outs):
        copy_in.wait()
        copy_out.start()
    for copy in outs:
        copy.wait()


def run_handed(place, slots, panels, earlier):
    hbm, smem = pl.BlockSpec(memory_space=pltpu.HBM), pl.BlockSpec(memory_space=pltpu.SMEM)
    return pl.pallas_call(
        handed_kernel,
        out_shape=[jax.ShapeDtypeStruct(p.shape[1:], p.dtype) for p in panels],
        in_specs=[smem, smem] + [hbm] * (len(panels) + 1),
        out_specs=[hbm] * len(panels),
        scratch_shapes=[pltpu.VMEM(p.shape[1:], p.dtype) for p in panels]
        + [pltpu.SemaphoreType.DMA((2 * len(panels),))],
        compiler_params=LARGE,
        cost_estimate=pl.CostEstimate(flops=0, bytes_accessed=2 * len(panels) * 2**20, transcendentals=0),
        name="handed",
    )(place, slots, *panels, earlier)


def swapped_kernel(place, slots, *refs):
    slot = slots[place[4]]
    ins, outs = [], []
    for k in range(3):
        panel, taken, out, room = refs[k], refs[3 + k], refs[6 + k], refs[9 + k]
        for j, source, at in ((0, panel.at[1 - slot], 1 - slot), (1, taken, slot)):
            ins.append(pltpu.make_async_copy(source, room.at[j], refs[12].at[2 * k + j]))
            outs.append(pltpu.make_async_copy(room.at[j], out.at[at], refs[12].at[6 + 2 * k + j]))
    for copy in ins:
        copy.start()
    for copy_in, copy_out in zip(ins, outs):
        copy_in.wait()
        copy_out.start()
    for copy in outs:
        copy.wait()


def run_swapped(place, slots, panels, taken):
    hbm = pl.BlockSpec(memory_space=pltpu.HBM)
    return pl.pallas_call(
        swapped_kernel,
        out_shape=[jax.ShapeDtypeStruct(p.shape, p.dtype) for p in panels],
        in_specs=[pl.BlockSpec(memory_space=pltpu.SMEM)] * 2 + [hbm] * 6,
        out_specs=[hbm] * 3,
        scratch_shapes=[pltpu.VMEM(p.shape, p.dtype) for p in panels] + [pltpu.SemaphoreType.DMA((12,))],
        compiler_params=LARGE,
        cost_estimate=pl.CostEstimate(flops=0, bytes_accessed=11 * 2**20, transcendentals=0),
        name="swapped",
    )(place, slots, *panels, *taken)


def layer_kernel(place, position_ref, *refs):
    piece0, pieces1 = refs[0], refs[1:5]
    gate_own, up_own, down_own, gate_other, up_other, down_other = refs[5:11]
    out0, outs1, count_ref = refs[11], refs[12:16], refs[16]
    rows_ref, panel_ref, down_ref, hidden_ref, result_ref, sems = refs[17:]
    my_x, my_core, chip = place[0], place[1], place[2]
    span = 2 * GROUP

    copies = []
    for q, (gate_w, up_w, slot) in enumerate(
        ((gate_own, up_own, 0), (gate_own, up_own, 1), (gate_other, up_other, 0), (gate_other, up_other, 1))
    ):
        copies.append(
            [
                pltpu.make_async_copy(gate_w.at[slot], panel_ref.at[q, :, :WIDTH, :128], sems.at[2 * q]),
                pltpu.make_async_copy(up_w.at[slot], panel_ref.at[q, :, :WIDTH, 128:], sems.at[2 * q + 1]),
            ]
        )
    copies.append([pltpu.make_async_copy(down_own, down_ref.at[:2], sems.at[8])])
    copies.append([pltpu.make_async_copy(down_other, down_ref.at[2:], sems.at[9])])
    for copy in copies[0] + copies[1]:
        copy.start()

    for q in range(4):
        panel_ref[q, :, WIDTH:, :] = jnp.zeros((8, LANES - WIDTH, 256), jnp.bfloat16)
    for xr in range(4):
        x_at = lax.rem(my_x - xr + 4, 4)
        lanes = pl.ds(pl.multiple_of(x_at * 2 * LANES, 2 * LANES), 2 * LANES)
        for zr in range(8):
            rows_ref[zr * span : (zr + 1) * span, lanes] = piece0[zr, xr]
            rows_ref[(8 + zr) * span : (9 + zr) * span, lanes] = pieces1[xr][zr]

    gates = rows_ref[:, WIDTH:LANES].astype(jnp.float32) * 256.0
    gates = gates + rows_ref[:, LANES + WIDTH : 2 * LANES].astype(jnp.float32)
    count_ref[...] = jnp.broadcast_to(
        jnp.sum((gates[8 * span :] > 0.0).astype(jnp.float32), axis=0, keepdims=True), count_ref.shape
    )
    positions = position_ref[...]
    for q in range(4):
        stored = chip * 4 + (my_core if q < 2 else 1 - my_core) * 2 + q % 2
        share = jnp.sum(jnp.where(positions == stored, gates, 0.0), axis=1, keepdims=True) * (1.0 / 65536.0)
        for copy in copies[q]:
            copy.wait()
        for copy in copies[q + 2]:
            copy.start()
        for step in range(2):
            at = slice(step * 256, (step + 1) * 256)
            act = jnp.zeros((256, 256), jnp.float32)
            for block in range(8):
                act = act + jnp.dot(
                    rows_ref[at, block * LANES : (block + 1) * LANES],
                    panel_ref[q, block],
                    preferred_element_type=jnp.float32,
                )
            value = jax.nn.silu(act[:, :128]) * act[:, 128:] * share[at]
            hidden_ref[at, q * 128 : (q + 1) * 128] = value.astype(jnp.bfloat16)
    for group in copies[4:]:
        for copy in group:
            copy.wait()
    for x_at in range(4):
        panel = down_ref[:, :, x_at * PAIR : (x_at + 1) * PAIR].reshape(4 * 128, PAIR)
        result_ref[x_at] = jnp.dot(hidden_ref[...], panel, preferred_element_type=jnp.float32).astype(jnp.bfloat16)

    for xr in range(4):
        x_at = lax.rem(my_x - xr + 4, 4)
        for zr in range(8):
            out0[zr, xr] = result_ref[x_at, zr * span : (zr + 1) * span, :]
            outs1[xr][zr] = result_ref[x_at, (8 + zr) * span : (9 + zr) * span, :]


def run_layer(place, position, piece0, pieces1, weights):
    vmem = pl.BlockSpec(memory_space=pltpu.VMEM)
    out = pl.pallas_call(
        layer_kernel,
        out_shape=[jax.ShapeDtypeStruct((8, 4, 2 * GROUP, PAIR), jnp.bfloat16)]
        + [jax.ShapeDtypeStruct((8, 2 * GROUP, PAIR), jnp.bfloat16)] * 4
        + [jax.ShapeDtypeStruct((8, 64), jnp.float32)],
        in_specs=[pl.BlockSpec(memory_space=pltpu.SMEM)]
        + [vmem] * 6
        + [pl.BlockSpec(memory_space=pltpu.HBM)] * 6,
        out_specs=[vmem] * 6,
        scratch_shapes=[
            pltpu.VMEM((512, 8 * LANES), jnp.bfloat16),
            pltpu.VMEM((4, 8, LANES, 256), jnp.bfloat16),
            pltpu.VMEM((4, 128, 3584), jnp.bfloat16),
            pltpu.VMEM((512, 512), jnp.bfloat16),
            pltpu.VMEM((4, 512, PAIR), jnp.bfloat16),
            pltpu.SemaphoreType.DMA((10,)),
        ],
        compiler_params=pltpu.CompilerParams(vmem_limit_bytes=52 * 2**20),
        cost_estimate=pl.CostEstimate(flops=2 * 512 * 3584 * 1536, bytes_accessed=20 * 2**20, transcendentals=0),
        name="layer",
    )(place, position, piece0, *pieces1, *weights)
    return out[0], out[1:5], out[5]


def on_device(tokens, routes, gate_fix, position, swap_slot, w_gate, w_up, w_down):
    yh, z, core = (lax.axis_index(a) for a in EXPERT_AXES)
    x, yl = (lax.axis_index(a) for a in DP_AXES)
    own_index = (yh * 8 + z) * 2 + core
    my_y = yh * 2 + yl
    place = jnp.stack([x, core, yh * 8 + z, my_y, own_index]).astype(jnp.int32)
    swap_core, swap_y = [(0, 1), (1, 0)], [(0, 1), (1, 0)]

    panels = (w_gate.reshape(2, 8, WIDTH, 128), w_up.reshape(2, 8, WIDTH, 128), w_down)
    other = tuple(lax.ppermute(w, "core", swap_core) for w in panels)
    weights = panels + other

    lower = run_ride(place, tokens, routes, gate_fix)
    step_rows = run_merge(place, after(gather_ring(lower, Y), other[0]))
    (gate_given,) = run_handed(place, swap_slot, panels[:1], lower)
    from_x = after(gather_ring(step_rows[0], "x"), other[1], gate_given)
    gate_taken = lax.ppermute(after(gate_given, *step_rows), "yh", swap_y)
    piece0 = lax.all_gather(jnp.stack(from_x), "z")
    up_given, down_given = run_handed(place, swap_slot, panels[1:], step_rows[1])
    over_z = gather_z(step_rows[1], (up_given, down_given))
    up_taken = lax.ppermute(after(up_given, gate_taken, over_z), "yh", swap_y)
    down_taken = lax.ppermute(after(down_given, up_taken), "yh", swap_y)
    pieces1 = gather_ring(over_z, "x")
    out0, out1, counts = run_layer(after(place, up_taken), position.reshape(1, 64), piece0, pieces1, weights)
    new = run_swapped(place, swap_slot, panels, (gate_taken, up_taken, down_taken))

    back0 = lax.psum_scatter(out0, "z", scatter_dimension=0)
    back0 = after(back0, *new)
    back1 = reduce_ring(out1, "x")
    back1 = reduce_z(back1)
    back0 = reduce_ring([back0[k] for k in range(4)], "x")
    back = jnp.stack([back0, back1]).reshape(2, 2, GROUP, PAIR)
    halves = [back[:, 0, :, :WIDTH], back[:, 0, :, WIDTH:], back[:, 1, :, :WIDTH], back[:, 1, :, WIDTH:]]
    combined = reduce_ring([lax.select_n(lax.rem(my_y - k + 4, 4), *halves) for k in range(4)], Y)

    counts = counts[0] + lax.ppermute(counts[0], "core", swap_core)
    holder, held_slot = position // 2, position % 2
    partner = jnp.bitwise_xor(holder, 16)
    owners = jnp.arange(32, dtype=jnp.int32)
    slot_of = lambda h: jnp.sum(jnp.where(h[:, None] == owners, swap_slot, 0), axis=1)
    new_holder = jnp.where(held_slot == slot_of(holder), partner, holder)
    device_load = (jnp.sum(jnp.where(new_holder == own_index, counts, 0.0)) / 128.0).reshape(1)

    return (combined, device_load, *[n.reshape(w.shape) for n, w in zip(new, (w_gate, w_up, w_down))])


def solution(mesh):
    fine = Mesh(mesh.devices.reshape(tuple(SIZES.values())), tuple(SIZES))
    in_specs = (
        P(None, EXPERT_AXES, DP_AXES),
        P(None, EXPERT_AXES, None),
        P(None, EXPERT_AXES, None),
        P(),
        P(),
        P(EXPERT_AXES, None, DP_AXES),
        P(EXPERT_AXES, None, DP_AXES),
        P(EXPERT_AXES, DP_AXES, None),
    )
    out_specs = (
        P(None, EXPERT_AXES, DP_AXES),
        P(EXPERT_AXES),
        P(EXPERT_AXES, None, DP_AXES),
        P(EXPERT_AXES, None, DP_AXES),
        P(EXPERT_AXES, DP_AXES, None),
    )
    return jax.shard_map(on_device, mesh=fine, in_specs=in_specs, out_specs=out_specs, check_vma=False)
```

```python
import functools

import jax
import jax.numpy as jnp
import numpy as np
from jax import lax
from jax.experimental import pallas as pl
from jax.experimental.pallas import tpu as pltpu
from jax.sharding import Mesh, PartitionSpec as P

SIZES = {"yh": 2, "z": 8, "core": 2, "x": 4, "yl": 2}
EXPERT_AXES = ("yh", "z", "core")
DP_AXES = ("x", "yl")
Y = ("yh", "yl")
GROUP = 16
WIDTH = 448
PAIR = 2 * WIDTH
LANES = 512
LARGE = pltpu.CompilerParams(vmem_limit_bytes=60 * 2**20)
SMALL = pltpu.CompilerParams(vmem_limit_bytes=4 * 2**20)


def ring_size(axes):
    return int(np.prod([SIZES[a] for a in axes]))


def send(value, axes, amount):
    count = ring_size(axes)
    return lax.ppermute(value, axes, [(i, (i + amount) % count) for i in range(count)])


def total(values):
    return functools.reduce(jnp.add, [v.astype(jnp.float32) for v in values]).astype(jnp.bfloat16)


def after(value, *earlier):
    return lax.optimization_barrier((value, earlier))[0]


def gather_ring(value, axes):
    return [value] + [send(value, axes, k) for k in range(1, ring_size(axes))]


def reduce_ring(pieces, axes):
    return total([pieces[0]] + [send(piece, axes, -k) for k, piece in enumerate(pieces) if k])


def gather_zx(value, beside):
    first = [send(value, "z", 1), send(value, "z", -1), send(value, "z", 4)]
    back, ahead, far = after(first, *beside)
    back2 = send(jnp.stack([value, back]), "z", 2)
    ahead2 = send(jnp.stack([value, ahead]), "z", -2)
    early = run_join([value[None], back[None], ahead[None], far[None]])
    before, behind = send(early, "x", 1), send(early, "x", -1)
    late = after(run_join([back2, ahead2]), before, behind)
    both = run_join([early, late])
    return both, ((both,), (before, send(late, "x", 1)), (send(both, "x", 2),), (behind, send(late, "x", -1)))


def run_join(parts):
    vmem = pl.BlockSpec(memory_space=pltpu.VMEM)

    def join_kernel(*refs):
        at = 0
        for ref in refs[:-1]:
            refs[-1][at : at + ref.shape[0]] = ref[...]
            at += ref.shape[0]

    count = sum(p.shape[0] for p in parts)
    return pl.pallas_call(
        join_kernel,
        out_shape=jax.ShapeDtypeStruct((count,) + parts[0].shape[1:], parts[0].dtype),
        in_specs=[vmem] * len(parts),
        out_specs=vmem,
        compiler_params=SMALL,
        name="join",
    )(*parts)


def reduce_z(pieces):
    back2 = send(pieces[4:6], "z", -2)
    ahead2 = send(pieces[6:8], "z", 2)
    far = send(pieces[3], "z", -4)
    back = send(total([pieces[1], back2[1]]), "z", -1)
    ahead = send(total([pieces[2], ahead2[1]]), "z", 1)
    return total([pieces[0], back2[0], ahead2[0], far, back, ahead])


def ride_kernel(place, tokens_ref, routes_ref, gate_ref, out_ref):
    labels = lax.broadcasted_iota(jnp.int32, (LANES - WIDTH, GROUP), 0)
    turn = (
        lax.broadcasted_iota(jnp.int32, (GROUP, GROUP), 0) == lax.broadcasted_iota(jnp.int32, (GROUP, GROUP), 1)
    ).astype(jnp.bfloat16)
    for step in range(2):
        gate, routes = gate_ref[step], routes_ref[step]
        part = jnp.where(lax.rem(place[3], 2) == 0, gate >> 8, gate & 255)
        ride = jnp.zeros(labels.shape, jnp.int32)
        for k in range(routes.shape[0]):
            ride = ride + jnp.where(routes[k : k + 1] == labels, part[k : k + 1], 0)
        ride = ride.astype(jnp.float32).astype(jnp.bfloat16)
        ride = lax.dot_general(turn, ride, (((1,), (1,)), ((), ())), preferred_element_type=jnp.float32)
        out_ref[step] = jnp.concatenate([tokens_ref[step], ride.astype(jnp.bfloat16)], axis=1)


def run_ride(place, tokens, routes, gate_fix):
    vmem = pl.BlockSpec(memory_space=pltpu.VMEM)
    return pl.pallas_call(
        ride_kernel,
        out_shape=jax.ShapeDtypeStruct((2, GROUP, LANES), jnp.bfloat16),
        in_specs=[pl.BlockSpec(memory_space=pltpu.SMEM)] + [vmem] * 3,
        out_specs=vmem,
        compiler_params=SMALL,
        name="ride",
    )(place, tokens, routes.transpose(0, 2, 1), gate_fix.transpose(0, 2, 1))


def merge_kernel(place, *refs):
    for k in range(4):
        y_at = lax.rem(place[3] - k + 4, 4)
        row = pl.multiple_of(lax.div(y_at, 2) * GROUP, GROUP)
        lane = pl.multiple_of(lax.rem(y_at, 2) * LANES, LANES)
        for step in range(2):
            refs[4 + step][pl.ds(row, GROUP), pl.ds(lane, LANES)] = refs[k][step]


def run_merge(place, from_y):
    vmem = pl.BlockSpec(memory_space=pltpu.VMEM)
    return pl.pallas_call(
        merge_kernel,
        out_shape=[jax.ShapeDtypeStruct((2 * GROUP, 2 * LANES), jnp.bfloat16)] * 2,
        in_specs=[pl.BlockSpec(memory_space=pltpu.SMEM)] + [vmem] * 4,
        out_specs=[vmem] * 2,
        compiler_params=SMALL,
        name="merge",
    )(place, *from_y)


def handed_kernel(place, slots, *refs):
    count = (len(refs) - 2) // 3
    slot, sems = slots[place[4]], refs[-1]
    ins = [pltpu.make_async_copy(refs[k].at[slot], refs[2 * count + 1 + k], sems.at[k]) for k in range(count)]
    outs = [pltpu.make_async_copy(refs[2 * count + 1 + k], refs[count + 1 + k], sems.at[count + k]) for k in range(count)]
    for copy in ins:
        copy.start()
    for copy_in, copy_out in zip(ins, outs):
        copy_in.wait()
        copy_out.start()
    for copy in outs:
        copy.wait()


def run_handed(place, slots, panels, earlier):
    hbm, smem = pl.BlockSpec(memory_space=pltpu.HBM), pl.BlockSpec(memory_space=pltpu.SMEM)
    return pl.pallas_call(
        handed_kernel,
        out_shape=[jax.ShapeDtypeStruct(p.shape[1:], p.dtype) for p in panels],
        in_specs=[smem, smem] + [hbm] * (len(panels) + 1),
        out_specs=[hbm] * len(panels),
        scratch_shapes=[pltpu.VMEM(p.shape[1:], p.dtype) for p in panels]
        + [pltpu.SemaphoreType.DMA((2 * len(panels),))],
        compiler_params=LARGE,
        cost_estimate=pl.CostEstimate(flops=0, bytes_accessed=2 * len(panels) * 2**20, transcendentals=0),
        name="handed",
    )(place, slots, *panels, earlier)


def swapped_kernel(place, slots, *refs):
    slot = slots[place[4]]
    ins, outs = [], []
    for k in range(3):
        panel, taken, out, room = refs[k], refs[3 + k], refs[6 + k], refs[9 + k]
        for j, source, at in ((0, panel.at[1 - slot], 1 - slot), (1, taken, slot)):
            ins.append(pltpu.make_async_copy(source, room.at[j], refs[12].at[2 * k + j]))
            outs.append(pltpu.make_async_copy(room.at[j], out.at[at], refs[12].at[6 + 2 * k + j]))
    for copy in ins:
        copy.start()
    for copy_in, copy_out in zip(ins, outs):
        copy_in.wait()
        copy_out.start()
    for copy in outs:
        copy.wait()


def run_swapped(place, slots, panels, taken):
    hbm = pl.BlockSpec(memory_space=pltpu.HBM)
    return pl.pallas_call(
        swapped_kernel,
        out_shape=[jax.ShapeDtypeStruct(p.shape, p.dtype) for p in panels],
        in_specs=[pl.BlockSpec(memory_space=pltpu.SMEM)] * 2 + [hbm] * 6,
        out_specs=[hbm] * 3,
        scratch_shapes=[pltpu.VMEM(p.shape, p.dtype) for p in panels] + [pltpu.SemaphoreType.DMA((12,))],
        compiler_params=LARGE,
        cost_estimate=pl.CostEstimate(flops=0, bytes_accessed=11 * 2**20, transcendentals=0),
        name="swapped",
    )(place, slots, *panels, *taken)


def layer_kernel(place, position_ref, *refs):
    piece0, pieces1 = refs[0], ((refs[1],), refs[2:4], (refs[4],), refs[5:7])
    gate_own, up_own, down_own, gate_other, up_other, down_other = refs[7:13]
    out0, outs1, count_ref = refs[13], refs[14:18], refs[18]
    rows_ref, gate_ref, up_ref, down_ref, hidden_ref, result_ref, sems = refs[19:]
    my_x, my_core, chip = place[0], place[1], place[2]
    span = 2 * GROUP

    copies = []
    for q, (gate_w, up_w, slot) in enumerate(
        ((gate_own, up_own, 0), (gate_own, up_own, 1), (gate_other, up_other, 0), (gate_other, up_other, 1))
    ):
        copies.append(
            [
                pltpu.make_async_copy(gate_w.at[slot], gate_ref.at[q, :, :WIDTH], sems.at[2 * q]),
                pltpu.make_async_copy(up_w.at[slot], up_ref.at[q, :, :WIDTH], sems.at[2 * q + 1]),
            ]
        )
    copies.append([pltpu.make_async_copy(down_own, down_ref.at[:2], sems.at[8])])
    copies.append([pltpu.make_async_copy(down_other, down_ref.at[2:], sems.at[9])])
    for copy in copies[0] + copies[1]:
        copy.start()

    for q in range(4):
        gate_ref[q, :, WIDTH:, :] = jnp.zeros((8, LANES - WIDTH, 128), jnp.bfloat16)
        up_ref[q, :, WIDTH:, :] = jnp.zeros((8, LANES - WIDTH, 128), jnp.bfloat16)
    for xr in range(4):
        x_at = lax.rem(my_x - xr + 4, 4)
        lanes = pl.ds(pl.multiple_of(x_at * 2 * LANES, 2 * LANES), 2 * LANES)
        for zr in range(8):
            rows_ref[zr * span : (zr + 1) * span, lanes] = piece0[zr, xr]
            part = pieces1[xr][zr // pieces1[xr][0].shape[0]]
            rows_ref[(8 + zr) * span : (9 + zr) * span, lanes] = part[zr % part.shape[0]]

    gates = rows_ref[:, WIDTH:LANES].astype(jnp.float32) * 256.0
    gates = gates + rows_ref[:, LANES + WIDTH : 2 * LANES].astype(jnp.float32)
    count_ref[...] = jnp.broadcast_to(
        jnp.sum((gates[8 * span :] > 0.0).astype(jnp.float32), axis=0, keepdims=True), count_ref.shape
    )
    positions = position_ref[...]
    for q in range(4):
        stored = chip * 4 + (my_core if q < 2 else 1 - my_core) * 2 + q % 2
        share = jnp.sum(jnp.where(positions == stored, gates, 0.0), axis=1, keepdims=True) * (1.0 / 65536.0)
        for copy in copies[q]:
            copy.wait()
        for copy in copies[q + 2]:
            copy.start()
        for step in range(2):
            at = slice(step * 256, (step + 1) * 256)
            act = jnp.zeros((256, 256), jnp.float32)
            for block in range(8):
                act = act + jnp.dot(
                    rows_ref[at, block * LANES : (block + 1) * LANES],
                    jnp.concatenate([gate_ref[q, block], up_ref[q, block]], axis=1),
                    preferred_element_type=jnp.float32,
                )
            value = jax.nn.silu(act[:, :128]) * act[:, 128:] * share[at]
            hidden_ref[at, q * 128 : (q + 1) * 128] = value.astype(jnp.bfloat16)
    for group in copies[4:]:
        for copy in group:
            copy.wait()
    for x_at in range(4):
        panel = down_ref[:, :, x_at * PAIR : (x_at + 1) * PAIR].reshape(4 * 128, PAIR)
        result_ref[x_at] = jnp.dot(hidden_ref[...], panel, preferred_element_type=jnp.float32).astype(jnp.bfloat16)

    for xr in range(4):
        x_at = lax.rem(my_x - xr + 4, 4)
        for zr in range(8):
            out0[zr, xr] = result_ref[x_at, zr * span : (zr + 1) * span, :]
            outs1[xr][zr] = result_ref[x_at, (8 + zr) * span : (9 + zr) * span, :]


def run_layer(place, position, piece0, pieces1, weights):
    vmem = pl.BlockSpec(memory_space=pltpu.VMEM)
    out = pl.pallas_call(
        layer_kernel,
        out_shape=[jax.ShapeDtypeStruct((8, 4, 2 * GROUP, PAIR), jnp.bfloat16)]
        + [jax.ShapeDtypeStruct((8, 2 * GROUP, PAIR), jnp.bfloat16)] * 4
        + [jax.ShapeDtypeStruct((8, 64), jnp.float32)],
        in_specs=[pl.BlockSpec(memory_space=pltpu.SMEM)]
        + [vmem] * 8
        + [pl.BlockSpec(memory_space=pltpu.HBM)] * 6,
        out_specs=[vmem] * 6,
        scratch_shapes=[
            pltpu.VMEM((512, 8 * LANES), jnp.bfloat16),
            pltpu.VMEM((4, 8, LANES, 128), jnp.bfloat16),
            pltpu.VMEM((4, 8, LANES, 128), jnp.bfloat16),
            pltpu.VMEM((4, 128, 3584), jnp.bfloat16),
            pltpu.VMEM((512, 512), jnp.bfloat16),
            pltpu.VMEM((4, 512, PAIR), jnp.bfloat16),
            pltpu.SemaphoreType.DMA((10,)),
        ],
        compiler_params=pltpu.CompilerParams(vmem_limit_bytes=52 * 2**20),
        cost_estimate=pl.CostEstimate(flops=2 * 512 * 3584 * 1536, bytes_accessed=20 * 2**20, transcendentals=0),
        name="layer",
    )(place, position, piece0, *sum(pieces1, ()), *weights)
    return out[0], out[1:5], out[5]


def on_device(tokens, routes, gate_fix, position, swap_slot, w_gate, w_up, w_down):
    yh, z, core = (lax.axis_index(a) for a in EXPERT_AXES)
    x, yl = (lax.axis_index(a) for a in DP_AXES)
    own_index = (yh * 8 + z) * 2 + core
    my_y = yh * 2 + yl
    place = jnp.stack([x, core, yh * 8 + z, my_y, own_index]).astype(jnp.int32)
    swap_core, swap_y = [(0, 1), (1, 0)], [(0, 1), (1, 0)]

    panels = (w_gate.reshape(2, 8, WIDTH, 128), w_up.reshape(2, 8, WIDTH, 128), w_down)
    other = tuple(lax.ppermute(w, "core", swap_core) for w in panels)
    weights = panels + other

    lower = run_ride(place, tokens, routes, gate_fix)
    step_rows = run_merge(place, after(gather_ring(lower, Y), other[0]))
    (gate_given,) = run_handed(place, swap_slot, panels[:1], lower)
    from_x = after(gather_ring(step_rows[0], "x"), other[1], gate_given)
    gate_taken = lax.ppermute(after(gate_given, *step_rows), "yh", swap_y)
    piece0 = lax.all_gather(jnp.stack(from_x), "z")
    up_given, down_given = run_handed(place, swap_slot, panels[1:], step_rows[1])
    over_z, pieces1 = gather_zx(step_rows[1], (up_given, down_given, other[2]))
    up_taken = lax.ppermute(after(up_given, gate_taken, over_z), "yh", swap_y)
    down_taken = lax.ppermute(after(down_given, up_taken), "yh", swap_y)
    out0, out1, counts = run_layer(after(place, up_taken), position.reshape(1, 64), piece0, pieces1, weights)
    new = run_swapped(place, swap_slot, panels, (gate_taken, up_taken, down_taken))

    back0 = lax.psum_scatter(out0, "z", scatter_dimension=0)
    back0 = after(back0, *new)
    back1 = reduce_ring(out1, "x")
    back1 = reduce_z(back1)
    back0 = reduce_ring([back0[k] for k in range(4)], "x")
    back = jnp.stack([back0, back1]).reshape(2, 2, GROUP, PAIR)
    halves = [back[:, 0, :, :WIDTH], back[:, 0, :, WIDTH:], back[:, 1, :, :WIDTH], back[:, 1, :, WIDTH:]]
    combined = reduce_ring([lax.select_n(lax.rem(my_y - k + 4, 4), *halves) for k in range(4)], Y)

    counts = counts[0] + lax.ppermute(counts[0], "core", swap_core)
    holder, held_slot = position // 2, position % 2
    partner = jnp.bitwise_xor(holder, 16)
    owners = jnp.arange(32, dtype=jnp.int32)
    slot_of = lambda h: jnp.sum(jnp.where(h[:, None] == owners, swap_slot, 0), axis=1)
    new_holder = jnp.where(held_slot == slot_of(holder), partner, holder)
    device_load = (jnp.sum(jnp.where(new_holder == own_index, counts, 0.0)) / 128.0).reshape(1)

    return (combined, device_load, *[n.reshape(w.shape) for n, w in zip(new, (w_gate, w_up, w_down))])


def solution(mesh):
    fine = Mesh(mesh.devices.reshape(tuple(SIZES.values())), tuple(SIZES))
    in_specs = (
        P(None, EXPERT_AXES, DP_AXES),
        P(None, EXPERT_AXES, None),
        P(None, EXPERT_AXES, None),
        P(),
        P(),
        P(EXPERT_AXES, None, DP_AXES),
        P(EXPERT_AXES, None, DP_AXES),
        P(EXPERT_AXES, DP_AXES, None),
    )
    out_specs = (
        P(None, EXPERT_AXES, DP_AXES),
        P(EXPERT_AXES),
        P(EXPERT_AXES, None, DP_AXES),
        P(EXPERT_AXES, None, DP_AXES),
        P(EXPERT_AXES, DP_AXES, None),
    )
    return jax.shard_map(on_device, mesh=fine, in_specs=in_specs, out_specs=out_specs, check_vma=False)
```

```python
import functools

import jax
import jax.numpy as jnp
import numpy as np
from jax import lax
from jax.experimental import pallas as pl
from jax.experimental.pallas import tpu as pltpu
from jax.sharding import Mesh, PartitionSpec as P

SIZES = {"yh": 2, "z": 8, "core": 2, "x": 4, "yl": 2}
EXPERT_AXES = ("yh", "z", "core")
DP_AXES = ("x", "yl")
Y = ("yh", "yl")
GROUP = 16
WIDTH = 448
PAIR = 2 * WIDTH
LANES = 512
LARGE = pltpu.CompilerParams(vmem_limit_bytes=60 * 2**20)
SMALL = pltpu.CompilerParams(vmem_limit_bytes=4 * 2**20)


def ring_size(axes):
    return int(np.prod([SIZES[a] for a in axes]))


def send(value, axes, amount):
    count = ring_size(axes)
    return lax.ppermute(value, axes, [(i, (i + amount) % count) for i in range(count)])


def total(values):
    return functools.reduce(jnp.add, [v.astype(jnp.float32) for v in values]).astype(jnp.bfloat16)


def after(value, *earlier):
    return lax.optimization_barrier((value, earlier))[0]


def gather_ring(value, axes):
    return [value] + [send(value, axes, k) for k in range(1, ring_size(axes))]


def reduce_ring(pieces, axes):
    return total([pieces[0]] + [send(piece, axes, -k) for k, piece in enumerate(pieces) if k])


def gather_zx(value, beside):
    first = [send(value, "z", 1), send(value, "z", -1), send(value, "z", 4)]
    back, ahead, far = after(first, *beside)
    back2 = send(jnp.stack([value, back]), "z", 2)
    ahead2 = send(jnp.stack([value, ahead]), "z", -2)
    early = run_join([value[None], back[None], ahead[None], far[None]])
    before, behind = send(early, "x", 1), send(early, "x", -1)
    late = after(run_join([back2, ahead2]), before, behind)
    both = run_join([early, late])
    return both, ((both,), (before, send(late, "x", 1)), (send(both, "x", 2),), (behind, send(late, "x", -1)))


def run_join(parts):
    vmem = pl.BlockSpec(memory_space=pltpu.VMEM)

    def join_kernel(*refs):
        at = 0
        for ref in refs[:-1]:
            refs[-1][at : at + ref.shape[0]] = ref[...]
            at += ref.shape[0]

    count = sum(p.shape[0] for p in parts)
    return pl.pallas_call(
        join_kernel,
        out_shape=jax.ShapeDtypeStruct((count,) + parts[0].shape[1:], parts[0].dtype),
        in_specs=[vmem] * len(parts),
        out_specs=vmem,
        compiler_params=SMALL,
        name="join",
    )(*parts)


def reduce_zx(pieces):
    own, (near1, far1), (middle,), (near3, far3) = pieces
    far1, far3, middle_in = send(far1, "x", -1), send(far3, "x", 1), send(middle, "x", -2)
    late = total([own[3:], far1, middle_in[3:], far3])
    near1, near3 = send(after(near1, far1, far3), "x", -1), send(after(near3, far1, far3), "x", 1)
    back2, ahead2, far = send(late[1:3], "z", -2), send(late[3:], "z", 2), send(late[0], "z", -4)
    early = total([own[:3], near1, middle_in[:3], near3])
    back = send(total([early[1], back2[1]]), "z", -1)
    ahead = send(total([early[2], ahead2[1]]), "z", 1)
    return total([early[0], back2[0], ahead2[0], far, back, ahead]), late


def ride_kernel(place, tokens_ref, routes_ref, gate_ref, out_ref):
    labels = lax.broadcasted_iota(jnp.int32, (LANES - WIDTH, GROUP), 0)
    turn = (
        lax.broadcasted_iota(jnp.int32, (GROUP, GROUP), 0) == lax.broadcasted_iota(jnp.int32, (GROUP, GROUP), 1)
    ).astype(jnp.bfloat16)
    for step in range(2):
        gate, routes = gate_ref[step], routes_ref[step]
        part = jnp.where(lax.rem(place[3], 2) == 0, gate >> 8, gate & 255)
        ride = jnp.zeros(labels.shape, jnp.int32)
        for k in range(routes.shape[0]):
            ride = ride + jnp.where(routes[k : k + 1] == labels, part[k : k + 1], 0)
        ride = ride.astype(jnp.float32).astype(jnp.bfloat16)
        ride = lax.dot_general(turn, ride, (((1,), (1,)), ((), ())), preferred_element_type=jnp.float32)
        out_ref[step] = jnp.concatenate([tokens_ref[step], ride.astype(jnp.bfloat16)], axis=1)


def run_ride(place, tokens, routes, gate_fix):
    vmem = pl.BlockSpec(memory_space=pltpu.VMEM)
    return pl.pallas_call(
        ride_kernel,
        out_shape=jax.ShapeDtypeStruct((2, GROUP, LANES), jnp.bfloat16),
        in_specs=[pl.BlockSpec(memory_space=pltpu.SMEM)] + [vmem] * 3,
        out_specs=vmem,
        compiler_params=SMALL,
        name="ride",
    )(place, tokens, routes.transpose(0, 2, 1), gate_fix.transpose(0, 2, 1))


def merge_kernel(place, *refs):
    for k in range(4):
        y_at = lax.rem(place[3] - k + 4, 4)
        row = pl.multiple_of(lax.div(y_at, 2) * GROUP, GROUP)
        lane = pl.multiple_of(lax.rem(y_at, 2) * LANES, LANES)
        for step in range(2):
            refs[4 + step][pl.ds(row, GROUP), pl.ds(lane, LANES)] = refs[k][step]


def run_merge(place, from_y):
    vmem = pl.BlockSpec(memory_space=pltpu.VMEM)
    return pl.pallas_call(
        merge_kernel,
        out_shape=[jax.ShapeDtypeStruct((2 * GROUP, 2 * LANES), jnp.bfloat16)] * 2,
        in_specs=[pl.BlockSpec(memory_space=pltpu.SMEM)] + [vmem] * 4,
        out_specs=[vmem] * 2,
        compiler_params=SMALL,
        name="merge",
    )(place, *from_y)


def handed_kernel(place, slots, *refs):
    count = (len(refs) - 2) // 3
    slot, sems = slots[place[4]], refs[-1]
    ins = [pltpu.make_async_copy(refs[k].at[slot], refs[2 * count + 1 + k], sems.at[k]) for k in range(count)]
    outs = [pltpu.make_async_copy(refs[2 * count + 1 + k], refs[count + 1 + k], sems.at[count + k]) for k in range(count)]
    for copy in ins:
        copy.start()
    for copy_in, copy_out in zip(ins, outs):
        copy_in.wait()
        copy_out.start()
    for copy in outs:
        copy.wait()


def run_handed(place, slots, panels, earlier):
    hbm, smem = pl.BlockSpec(memory_space=pltpu.HBM), pl.BlockSpec(memory_space=pltpu.SMEM)
    return pl.pallas_call(
        handed_kernel,
        out_shape=[jax.ShapeDtypeStruct(p.shape[1:], p.dtype) for p in panels],
        in_specs=[smem, smem] + [hbm] * (len(panels) + 1),
        out_specs=[hbm] * len(panels),
        scratch_shapes=[pltpu.VMEM(p.shape[1:], p.dtype) for p in panels]
        + [pltpu.SemaphoreType.DMA((2 * len(panels),))],
        compiler_params=LARGE,
        cost_estimate=pl.CostEstimate(flops=0, bytes_accessed=2 * len(panels) * 2**20, transcendentals=0),
        name="handed",
    )(place, slots, *panels, earlier)


def swapped_kernel(place, slots, *refs):
    slot = slots[place[4]]
    ins, outs = [], []
    for k in range(3):
        panel, taken, out, room = refs[k], refs[3 + k], refs[6 + k], refs[9 + k]
        for j, source, at in ((0, panel.at[1 - slot], 1 - slot), (1, taken, slot)):
            ins.append(pltpu.make_async_copy(source, room.at[j], refs[12].at[2 * k + j]))
            outs.append(pltpu.make_async_copy(room.at[j], out.at[at], refs[12].at[6 + 2 * k + j]))
    for copy in ins:
        copy.start()
    for copy_in, copy_out in zip(ins, outs):
        copy_in.wait()
        copy_out.start()
    for copy in outs:
        copy.wait()


def run_swapped(place, slots, panels, taken):
    hbm = pl.BlockSpec(memory_space=pltpu.HBM)
    return pl.pallas_call(
        swapped_kernel,
        out_shape=[jax.ShapeDtypeStruct(p.shape, p.dtype) for p in panels],
        in_specs=[pl.BlockSpec(memory_space=pltpu.SMEM)] * 2 + [hbm] * 6,
        out_specs=[hbm] * 3,
        scratch_shapes=[pltpu.VMEM(p.shape, p.dtype) for p in panels] + [pltpu.SemaphoreType.DMA((12,))],
        compiler_params=LARGE,
        cost_estimate=pl.CostEstimate(flops=0, bytes_accessed=11 * 2**20, transcendentals=0),
        name="swapped",
    )(place, slots, *panels, *taken)


def layer_kernel(place, position_ref, *refs):
    piece0, pieces1 = refs[0], ((refs[1],), refs[2:4], (refs[4],), refs[5:7])
    gate_own, up_own, down_own, gate_other, up_other, down_other = refs[7:13]
    out0, outs1, count_ref = refs[13], ((refs[14],), refs[15:17], (refs[17],), refs[18:20]), refs[20]
    rows_ref, gate_ref, up_ref, down_ref, hidden_ref, result_ref, sems = refs[21:]
    my_x, my_core, chip = place[0], place[1], place[2]
    span = 2 * GROUP

    copies = []
    for q, (gate_w, up_w, slot) in enumerate(
        ((gate_own, up_own, 0), (gate_own, up_own, 1), (gate_other, up_other, 0), (gate_other, up_other, 1))
    ):
        copies.append(
            [
                pltpu.make_async_copy(gate_w.at[slot], gate_ref.at[q, :, :WIDTH], sems.at[2 * q]),
                pltpu.make_async_copy(up_w.at[slot], up_ref.at[q, :, :WIDTH], sems.at[2 * q + 1]),
            ]
        )
    copies.append([pltpu.make_async_copy(down_own, down_ref.at[:2], sems.at[8])])
    copies.append([pltpu.make_async_copy(down_other, down_ref.at[2:], sems.at[9])])
    for copy in copies[0] + copies[1]:
        copy.start()

    for q in range(4):
        gate_ref[q, :, WIDTH:, :] = jnp.zeros((8, LANES - WIDTH, 128), jnp.bfloat16)
        up_ref[q, :, WIDTH:, :] = jnp.zeros((8, LANES - WIDTH, 128), jnp.bfloat16)
    for xr in range(4):
        x_at = lax.rem(my_x - xr + 4, 4)
        lanes = pl.ds(pl.multiple_of(x_at * 2 * LANES, 2 * LANES), 2 * LANES)
        for zr in range(8):
            rows_ref[zr * span : (zr + 1) * span, lanes] = piece0[zr, xr]
            part = pieces1[xr][zr // pieces1[xr][0].shape[0]]
            rows_ref[(8 + zr) * span : (9 + zr) * span, lanes] = part[zr % part.shape[0]]

    gates = rows_ref[:, WIDTH:LANES].astype(jnp.float32) * 256.0
    gates = gates + rows_ref[:, LANES + WIDTH : 2 * LANES].astype(jnp.float32)
    count_ref[...] = jnp.broadcast_to(
        jnp.sum((gates[8 * span :] > 0.0).astype(jnp.float32), axis=0, keepdims=True), count_ref.shape
    )
    positions = position_ref[...]
    for q in range(4):
        stored = chip * 4 + (my_core if q < 2 else 1 - my_core) * 2 + q % 2
        share = jnp.sum(jnp.where(positions == stored, gates, 0.0), axis=1, keepdims=True) * (1.0 / 65536.0)
        for copy in copies[q]:
            copy.wait()
        for copy in copies[q + 2]:
            copy.start()
        for step in range(2):
            at = slice(step * 256, (step + 1) * 256)
            act = jnp.zeros((256, 256), jnp.float32)
            for block in range(8):
                act = act + jnp.dot(
                    rows_ref[at, block * LANES : (block + 1) * LANES],
                    jnp.concatenate([gate_ref[q, block], up_ref[q, block]], axis=1),
                    preferred_element_type=jnp.float32,
                )
            value = jax.nn.silu(act[:, :128]) * act[:, 128:] * share[at]
            hidden_ref[at, q * 128 : (q + 1) * 128] = value.astype(jnp.bfloat16)
    for group in copies[4:]:
        for copy in group:
            copy.wait()
    for x_at in range(4):
        panel = down_ref[:, :, x_at * PAIR : (x_at + 1) * PAIR].reshape(4 * 128, PAIR)
        result_ref[x_at] = jnp.dot(hidden_ref[...], panel, preferred_element_type=jnp.float32).astype(jnp.bfloat16)

    for xr in range(4):
        x_at = lax.rem(my_x - xr + 4, 4)
        for zr in range(8):
            out0[zr, xr] = result_ref[x_at, zr * span : (zr + 1) * span, :]
            whole = len(outs1[xr]) == 1
            out = outs1[xr][0 if whole or zr < 3 else 1]
            out[zr if whole or zr < 3 else zr - 3] = result_ref[x_at, (8 + zr) * span : (9 + zr) * span, :]


def run_layer(place, position, piece0, pieces1, weights):
    vmem = pl.BlockSpec(memory_space=pltpu.VMEM)
    out = pl.pallas_call(
        layer_kernel,
        out_shape=[jax.ShapeDtypeStruct((8, 4, 2 * GROUP, PAIR), jnp.bfloat16)]
        + [jax.ShapeDtypeStruct((n, 2 * GROUP, PAIR), jnp.bfloat16) for n in (8, 3, 5, 8, 3, 5)]
        + [jax.ShapeDtypeStruct((8, 64), jnp.float32)],
        in_specs=[pl.BlockSpec(memory_space=pltpu.SMEM)]
        + [vmem] * 8
        + [pl.BlockSpec(memory_space=pltpu.HBM)] * 6,
        out_specs=[vmem] * 8,
        scratch_shapes=[
            pltpu.VMEM((512, 8 * LANES), jnp.bfloat16),
            pltpu.VMEM((4, 8, LANES, 128), jnp.bfloat16),
            pltpu.VMEM((4, 8, LANES, 128), jnp.bfloat16),
            pltpu.VMEM((4, 128, 3584), jnp.bfloat16),
            pltpu.VMEM((512, 512), jnp.bfloat16),
            pltpu.VMEM((4, 512, PAIR), jnp.bfloat16),
            pltpu.SemaphoreType.DMA((10,)),
        ],
        compiler_params=pltpu.CompilerParams(vmem_limit_bytes=52 * 2**20),
        cost_estimate=pl.CostEstimate(flops=2 * 512 * 3584 * 1536, bytes_accessed=20 * 2**20, transcendentals=0),
        name="layer",
    )(place, position, piece0, *sum(pieces1, ()), *weights)
    return out[0], (out[1], out[2:4], out[4:5], out[5:7]), out[7]


def on_device(tokens, routes, gate_fix, position, swap_slot, w_gate, w_up, w_down):
    yh, z, core = (lax.axis_index(a) for a in EXPERT_AXES)
    x, yl = (lax.axis_index(a) for a in DP_AXES)
    own_index = (yh * 8 + z) * 2 + core
    my_y = yh * 2 + yl
    place = jnp.stack([x, core, yh * 8 + z, my_y, own_index]).astype(jnp.int32)
    swap_core, swap_y = [(0, 1), (1, 0)], [(0, 1), (1, 0)]

    panels = (w_gate.reshape(2, 8, WIDTH, 128), w_up.reshape(2, 8, WIDTH, 128), w_down)
    other = tuple(lax.ppermute(w, "core", swap_core) for w in panels)
    weights = panels + other

    lower = run_ride(place, tokens, routes, gate_fix)
    step_rows = run_merge(place, after(gather_ring(lower, Y), other[0]))
    (gate_given,) = run_handed(place, swap_slot, panels[:1], lower)
    from_x = after(gather_ring(step_rows[0], "x"), other[1], gate_given)
    gate_taken = lax.ppermute(after(gate_given, *step_rows), "yh", swap_y)
    piece0 = lax.all_gather(jnp.stack(from_x), "z")
    up_given, down_given = run_handed(place, swap_slot, panels[1:], step_rows[1])
    over_z, pieces1 = gather_zx(step_rows[1], (up_given, down_given, other[2]))
    up_taken = lax.ppermute(after(up_given, gate_taken, over_z), "yh", swap_y)
    down_taken = lax.ppermute(after(down_given, up_taken), "yh", swap_y)
    out0, out1, counts = run_layer(after(place, up_taken), position.reshape(1, 64), piece0, pieces1, weights)
    back1, late = reduce_zx(out1)
    new = run_swapped(place, swap_slot, panels, (gate_taken, up_taken, after(down_taken, late)))

    back0 = lax.psum_scatter(out0, "z", scatter_dimension=0)
    back0 = after(back0, *new)
    back0 = reduce_ring([back0[k] for k in range(4)], "x")
    back = jnp.stack([back0, back1]).reshape(2, 2, GROUP, PAIR)
    halves = [back[:, 0, :, :WIDTH], back[:, 0, :, WIDTH:], back[:, 1, :, :WIDTH], back[:, 1, :, WIDTH:]]
    combined = reduce_ring([lax.select_n(lax.rem(my_y - k + 4, 4), *halves) for k in range(4)], Y)

    counts = counts[0] + lax.ppermute(counts[0], "core", swap_core)
    holder, held_slot = position // 2, position % 2
    partner = jnp.bitwise_xor(holder, 16)
    owners = jnp.arange(32, dtype=jnp.int32)
    slot_of = lambda h: jnp.sum(jnp.where(h[:, None] == owners, swap_slot, 0), axis=1)
    new_holder = jnp.where(held_slot == slot_of(holder), partner, holder)
    device_load = (jnp.sum(jnp.where(new_holder == own_index, counts, 0.0)) / 128.0).reshape(1)

    return (combined, device_load, *[n.reshape(w.shape) for n, w in zip(new, (w_gate, w_up, w_down))])


def solution(mesh):
    fine = Mesh(mesh.devices.reshape(tuple(SIZES.values())), tuple(SIZES))
    in_specs = (
        P(None, EXPERT_AXES, DP_AXES),
        P(None, EXPERT_AXES, None),
        P(None, EXPERT_AXES, None),
        P(),
        P(),
        P(EXPERT_AXES, None, DP_AXES),
        P(EXPERT_AXES, None, DP_AXES),
        P(EXPERT_AXES, DP_AXES, None),
    )
    out_specs = (
        P(None, EXPERT_AXES, DP_AXES),
        P(EXPERT_AXES),
        P(EXPERT_AXES, None, DP_AXES),
        P(EXPERT_AXES, None, DP_AXES),
        P(EXPERT_AXES, DP_AXES, None),
    )
    return jax.shard_map(on_device, mesh=fine, in_specs=in_specs, out_specs=out_specs, check_vma=False)
```

```python
import functools

import jax
import jax.numpy as jnp
import numpy as np
from jax import lax
from jax.experimental import pallas as pl
from jax.experimental.pallas import tpu as pltpu
from jax.sharding import Mesh, PartitionSpec as P

SIZES = {"yh": 2, "z": 8, "core": 2, "x": 4, "yl": 2}
EXPERT_AXES = ("yh", "z", "core")
DP_AXES = ("x", "yl")
Y = ("yh", "yl")
GROUP = 16
WIDTH = 448
PAIR = 2 * WIDTH
LANES = 512
LARGE = pltpu.CompilerParams(vmem_limit_bytes=60 * 2**20)
SMALL = pltpu.CompilerParams(vmem_limit_bytes=4 * 2**20)


def ring_size(axes):
    return int(np.prod([SIZES[a] for a in axes]))


def send(value, axes, amount):
    count = ring_size(axes)
    return lax.ppermute(value, axes, [(i, (i + amount) % count) for i in range(count)])


def total(values):
    return functools.reduce(jnp.add, [v.astype(jnp.float32) for v in values]).astype(jnp.bfloat16)


def after(value, *earlier):
    return lax.optimization_barrier((value, earlier))[0]


def gather_ring(value, axes):
    return [value] + [send(value, axes, k) for k in range(1, ring_size(axes))]


def reduce_ring(pieces, axes):
    return total([pieces[0]] + [send(piece, axes, -k) for k, piece in enumerate(pieces) if k])


def gather_zx(value, beside):
    first = [send(value, "z", 1), send(value, "z", -1), send(value, "z", 4)]
    back, ahead, far = after(first, *beside)
    back2 = send(jnp.stack([value, back]), "z", 2)
    ahead2 = send(jnp.stack([value, ahead]), "z", -2)
    early = run_join([value[None], back[None], ahead[None], far[None]])
    over_x = gather_ring(early, "x")
    late = after(run_join([back2, ahead2]), *over_x)
    return late, tuple(zip(over_x, gather_ring(late, "x")))


def run_join(parts):
    vmem = pl.BlockSpec(memory_space=pltpu.VMEM)

    def join_kernel(*refs):
        at = 0
        for ref in refs[:-1]:
            refs[-1][at : at + ref.shape[0]] = ref[...]
            at += ref.shape[0]

    count = sum(p.shape[0] for p in parts)
    return pl.pallas_call(
        join_kernel,
        out_shape=jax.ShapeDtypeStruct((count,) + parts[0].shape[1:], parts[0].dtype),
        in_specs=[vmem] * len(parts),
        out_specs=vmem,
        compiler_params=SMALL,
        name="join",
    )(*parts)


def reduce_zx(pieces):
    own, (near1, far1), (middle,), (near3, far3) = pieces
    far1, far3, middle_in = send(far1, "x", -1), send(far3, "x", 1), send(middle, "x", -2)
    late = total([own[3:], far1, middle_in[3:], far3])
    near1, near3 = send(after(near1, far1, far3), "x", -1), send(after(near3, far1, far3), "x", 1)
    back2, ahead2, far = send(late[1:3], "z", -2), send(late[3:], "z", 2), send(late[0], "z", -4)
    early = total([own[:3], near1, middle_in[:3], near3])
    back = send(total([early[1], back2[1]]), "z", -1)
    ahead = send(total([early[2], ahead2[1]]), "z", 1)
    return total([early[0], back2[0], ahead2[0], far, back, ahead]), late


def ride_kernel(place, tokens_ref, routes_ref, gate_ref, out_ref):
    labels = lax.broadcasted_iota(jnp.int32, (LANES - WIDTH, GROUP), 0)
    turn = (
        lax.broadcasted_iota(jnp.int32, (GROUP, GROUP), 0) == lax.broadcasted_iota(jnp.int32, (GROUP, GROUP), 1)
    ).astype(jnp.bfloat16)
    for step in range(2):
        gate, routes = gate_ref[step], routes_ref[step]
        part = jnp.where(lax.rem(place[3], 2) == 0, gate >> 8, gate & 255)
        ride = jnp.zeros(labels.shape, jnp.int32)
        for k in range(routes.shape[0]):
            ride = ride + jnp.where(routes[k : k + 1] == labels, part[k : k + 1], 0)
        ride = ride.astype(jnp.float32).astype(jnp.bfloat16)
        ride = lax.dot_general(turn, ride, (((1,), (1,)), ((), ())), preferred_element_type=jnp.float32)
        out_ref[step] = jnp.concatenate([tokens_ref[step], ride.astype(jnp.bfloat16)], axis=1)


def run_ride(place, tokens, routes, gate_fix):
    vmem = pl.BlockSpec(memory_space=pltpu.VMEM)
    return pl.pallas_call(
        ride_kernel,
        out_shape=jax.ShapeDtypeStruct((2, GROUP, LANES), jnp.bfloat16),
        in_specs=[pl.BlockSpec(memory_space=pltpu.SMEM)] + [vmem] * 3,
        out_specs=vmem,
        compiler_params=SMALL,
        name="ride",
    )(place, tokens, routes.transpose(0, 2, 1), gate_fix.transpose(0, 2, 1))


def merge_kernel(place, *refs):
    for k in range(4):
        y_at = lax.rem(place[3] - k + 4, 4)
        row = pl.multiple_of(lax.div(y_at, 2) * GROUP, GROUP)
        lane = pl.multiple_of(lax.rem(y_at, 2) * LANES, LANES)
        for step in range(2):
            refs[4 + step][pl.ds(row, GROUP), pl.ds(lane, LANES)] = refs[k][step]


def run_merge(place, from_y):
    vmem = pl.BlockSpec(memory_space=pltpu.VMEM)
    return pl.pallas_call(
        merge_kernel,
        out_shape=[jax.ShapeDtypeStruct((2 * GROUP, 2 * LANES), jnp.bfloat16)] * 2,
        in_specs=[pl.BlockSpec(memory_space=pltpu.SMEM)] + [vmem] * 4,
        out_specs=[vmem] * 2,
        compiler_params=SMALL,
        name="merge",
    )(place, *from_y)


def swap_views(gate, up, down, slot, room):
    views = [(gate.at[slot], room.at[:3584]), (up.at[slot], room.at[3584:7168])]
    for c in range(28):
        views.append((down.at[slot, :, c * 128 : (c + 1) * 128], room.at[7168 + c * 128 : 7296 + c * 128]))
    return views


def handed_kernel(place, slots, gate, up, down, earlier_ref, out, room, sems):
    views = swap_views(gate, up, down, slots[place[4]], room)
    copies = [pltpu.make_async_copy(source, to, sems.at[k]) for k, (source, to) in enumerate(views)]
    for copy in copies:
        copy.start()
    for copy in copies:
        copy.wait()
    copy = pltpu.make_async_copy(room, out, sems.at[30])
    copy.start()
    copy.wait()


def run_handed(place, slots, panels, earlier):
    hbm, smem = pl.BlockSpec(memory_space=pltpu.HBM), pl.BlockSpec(memory_space=pltpu.SMEM)
    shape = (3 * 3584, 128)
    return pl.pallas_call(
        handed_kernel,
        out_shape=jax.ShapeDtypeStruct(shape, jnp.bfloat16),
        in_specs=[smem, smem] + [hbm] * 4,
        out_specs=hbm,
        scratch_shapes=[pltpu.VMEM(shape, jnp.bfloat16), pltpu.SemaphoreType.DMA((31,))],
        compiler_params=LARGE,
        cost_estimate=pl.CostEstimate(flops=0, bytes_accessed=6 * 2**20, transcendentals=0),
        name="handed",
    )(place, slots, *panels, earlier)


def swapped_kernel(place, slots, gate, up, down, taken, *refs):
    outs, kept_rooms, room, sems = refs[:3], refs[3:6], refs[6], refs[7]
    slot = slots[place[4]]
    arrive = [pltpu.make_async_copy(taken, room, sems.at[0])]
    leave = [[pltpu.make_async_copy(r, o, sems.at[7 + k]) for k, (o, r) in enumerate(swap_views(*outs, slot, room))]]
    for k, (panel, out, kept) in enumerate(zip((gate, up, down), outs, kept_rooms)):
        arrive.append(pltpu.make_async_copy(panel.at[1 - slot], kept, sems.at[1 + k]))
        leave.append([pltpu.make_async_copy(kept, out.at[1 - slot], sems.at[4 + k])])
    for copy in arrive:
        copy.start()
    for copy_in, copies_out in zip(arrive, leave):
        copy_in.wait()
        for copy in copies_out:
            copy.start()
    for copies_out in leave:
        for copy in copies_out:
            copy.wait()


def run_swapped(place, slots, panels, taken):
    hbm, smem = pl.BlockSpec(memory_space=pltpu.HBM), pl.BlockSpec(memory_space=pltpu.SMEM)
    return pl.pallas_call(
        swapped_kernel,
        out_shape=[jax.ShapeDtypeStruct(p.shape, p.dtype) for p in panels],
        in_specs=[smem, smem] + [hbm] * 4,
        out_specs=[hbm] * 3,
        scratch_shapes=[pltpu.VMEM(p.shape[1:], p.dtype) for p in panels]
        + [pltpu.VMEM(taken.shape, taken.dtype), pltpu.SemaphoreType.DMA((37,))],
        compiler_params=LARGE,
        cost_estimate=pl.CostEstimate(flops=0, bytes_accessed=11 * 2**20, transcendentals=0),
        name="swapped",
    )(place, slots, *panels, taken)


def layer_kernel(place, position_ref, *refs):
    piece0, pieces1 = refs[0], (refs[1:3], refs[3:5], refs[5:7], refs[7:9])
    gate_own, up_own, down_own, gate_other, up_other, down_other = refs[9:15]
    out0, outs1, count_ref = refs[15], ((refs[16],), refs[17:19], (refs[19],), refs[20:22]), refs[22]
    rows_ref, gate_ref, up_ref, down_ref, hidden_ref, result_ref, sems = refs[23:]
    my_x, my_core, chip = place[0], place[1], place[2]
    span = 2 * GROUP

    copies = []
    for q, (gate_w, up_w, slot) in enumerate(
        ((gate_own, up_own, 0), (gate_own, up_own, 1), (gate_other, up_other, 0), (gate_other, up_other, 1))
    ):
        copies.append(
            [
                pltpu.make_async_copy(gate_w.at[slot], gate_ref.at[q, :, :WIDTH], sems.at[2 * q]),
                pltpu.make_async_copy(up_w.at[slot], up_ref.at[q, :, :WIDTH], sems.at[2 * q + 1]),
            ]
        )
    copies.append([pltpu.make_async_copy(down_own, down_ref.at[:2], sems.at[8])])
    copies.append([pltpu.make_async_copy(down_other, down_ref.at[2:], sems.at[9])])
    for copy in copies[0] + copies[1]:
        copy.start()

    for q in range(4):
        gate_ref[q, :, WIDTH:, :] = jnp.zeros((8, LANES - WIDTH, 128), jnp.bfloat16)
        up_ref[q, :, WIDTH:, :] = jnp.zeros((8, LANES - WIDTH, 128), jnp.bfloat16)
    for xr in range(4):
        x_at = lax.rem(my_x - xr + 4, 4)
        lanes = pl.ds(pl.multiple_of(x_at * 2 * LANES, 2 * LANES), 2 * LANES)
        for zr in range(8):
            rows_ref[zr * span : (zr + 1) * span, lanes] = piece0[zr, xr]
            part = pieces1[xr][zr // pieces1[xr][0].shape[0]]
            rows_ref[(8 + zr) * span : (9 + zr) * span, lanes] = part[zr % part.shape[0]]

    gates = rows_ref[:, WIDTH:LANES].astype(jnp.float32) * 256.0
    gates = gates + rows_ref[:, LANES + WIDTH : 2 * LANES].astype(jnp.float32)
    count_ref[...] = jnp.broadcast_to(
        jnp.sum((gates[8 * span :] > 0.0).astype(jnp.float32), axis=0, keepdims=True), count_ref.shape
    )
    positions = position_ref[...]
    for q in range(4):
        stored = chip * 4 + (my_core if q < 2 else 1 - my_core) * 2 + q % 2
        share = jnp.sum(jnp.where(positions == stored, gates, 0.0), axis=1, keepdims=True) * (1.0 / 65536.0)
        for copy in copies[q]:
            copy.wait()
        for copy in copies[q + 2]:
            copy.start()
        for step in range(2):
            at = slice(step * 256, (step + 1) * 256)
            act = jnp.zeros((256, 256), jnp.float32)
            for block in range(8):
                act = act + jnp.dot(
                    rows_ref[at, block * LANES : (block + 1) * LANES],
                    jnp.concatenate([gate_ref[q, block], up_ref[q, block]], axis=1),
                    preferred_element_type=jnp.float32,
                )
            value = jax.nn.silu(act[:, :128]) * act[:, 128:] * share[at]
            hidden_ref[at, q * 128 : (q + 1) * 128] = value.astype(jnp.bfloat16)
    for group in copies[4:]:
        for copy in group:
            copy.wait()
    for x_at in range(4):
        panel = down_ref[:, :, x_at * PAIR : (x_at + 1) * PAIR].reshape(4 * 128, PAIR)
        result_ref[x_at] = jnp.dot(hidden_ref[...], panel, preferred_element_type=jnp.float32).astype(jnp.bfloat16)

    for xr in range(4):
        x_at = lax.rem(my_x - xr + 4, 4)
        for zr in range(8):
            out0[zr, xr] = result_ref[x_at, zr * span : (zr + 1) * span, :]
            whole = len(outs1[xr]) == 1
            out = outs1[xr][0 if whole or zr < 3 else 1]
            out[zr if whole or zr < 3 else zr - 3] = result_ref[x_at, (8 + zr) * span : (9 + zr) * span, :]


def run_layer(place, position, piece0, pieces1, weights):
    vmem = pl.BlockSpec(memory_space=pltpu.VMEM)
    out = pl.pallas_call(
        layer_kernel,
        out_shape=[jax.ShapeDtypeStruct((8, 4, 2 * GROUP, PAIR), jnp.bfloat16)]
        + [jax.ShapeDtypeStruct((n, 2 * GROUP, PAIR), jnp.bfloat16) for n in (8, 3, 5, 8, 3, 5)]
        + [jax.ShapeDtypeStruct((8, 64), jnp.float32)],
        in_specs=[pl.BlockSpec(memory_space=pltpu.SMEM)]
        + [vmem] * 10
        + [pl.BlockSpec(memory_space=pltpu.HBM)] * 6,
        out_specs=[vmem] * 8,
        scratch_shapes=[
            pltpu.VMEM((512, 8 * LANES), jnp.bfloat16),
            pltpu.VMEM((4, 8, LANES, 128), jnp.bfloat16),
            pltpu.VMEM((4, 8, LANES, 128), jnp.bfloat16),
            pltpu.VMEM((4, 128, 3584), jnp.bfloat16),
            pltpu.VMEM((512, 512), jnp.bfloat16),
            pltpu.VMEM((4, 512, PAIR), jnp.bfloat16),
            pltpu.SemaphoreType.DMA((10,)),
        ],
        compiler_params=pltpu.CompilerParams(vmem_limit_bytes=52 * 2**20),
        cost_estimate=pl.CostEstimate(flops=2 * 512 * 3584 * 1536, bytes_accessed=20 * 2**20, transcendentals=0),
        name="layer",
    )(place, position, piece0, *sum(pieces1, ()), *weights)
    return out[0], (out[1], out[2:4], out[4:5], out[5:7]), out[7]


def on_device(tokens, routes, gate_fix, position, swap_slot, w_gate, w_up, w_down):
    yh, z, core = (lax.axis_index(a) for a in EXPERT_AXES)
    x, yl = (lax.axis_index(a) for a in DP_AXES)
    own_index = (yh * 8 + z) * 2 + core
    my_y = yh * 2 + yl
    place = jnp.stack([x, core, yh * 8 + z, my_y, own_index]).astype(jnp.int32)
    swap_core, swap_y = [(0, 1), (1, 0)], [(0, 1), (1, 0)]

    panels = (w_gate.reshape(2, 8, WIDTH, 128), w_up.reshape(2, 8, WIDTH, 128), w_down)
    other = tuple(lax.ppermute(w, "core", swap_core) for w in panels)
    weights = panels + other

    lower = run_ride(place, tokens, routes, gate_fix)
    step_rows = run_merge(place, after(gather_ring(lower, Y), other[0]))
    whole = (w_gate, w_up, w_down)
    given = run_handed(place, swap_slot, whole, step_rows[1])
    from_x = after(gather_ring(step_rows[0], "x"), other[1])
    piece0 = lax.all_gather(jnp.stack(from_x), "z")
    over_z, pieces1 = gather_zx(step_rows[1], (given, other[2]))
    taken = lax.ppermute(after(given, over_z), "yh", swap_y)
    out0, out1, counts = run_layer(place, position.reshape(1, 64), piece0, pieces1, weights)
    back1, late = reduce_zx(out1)
    new = run_swapped(place, swap_slot, whole, after(taken, back1))

    back0 = lax.psum_scatter(out0, "z", scatter_dimension=0)
    back0 = after(back0, *new)
    back0 = reduce_ring([back0[k] for k in range(4)], "x")
    back = jnp.stack([back0, back1]).reshape(2, 2, GROUP, PAIR)
    halves = [back[:, 0, :, :WIDTH], back[:, 0, :, WIDTH:], back[:, 1, :, :WIDTH], back[:, 1, :, WIDTH:]]
    combined = reduce_ring([lax.select_n(lax.rem(my_y - k + 4, 4), *halves) for k in range(4)], Y)

    counts = counts[0] + lax.ppermute(counts[0], "core", swap_core)
    holder, held_slot = position // 2, position % 2
    partner = jnp.bitwise_xor(holder, 16)
    owners = jnp.arange(32, dtype=jnp.int32)
    slot_of = lambda h: jnp.sum(jnp.where(h[:, None] == owners, swap_slot, 0), axis=1)
    new_holder = jnp.where(held_slot == slot_of(holder), partner, holder)
    device_load = (jnp.sum(jnp.where(new_holder == own_index, counts, 0.0)) / 128.0).reshape(1)

    return (combined, device_load, *[n.reshape(w.shape) for n, w in zip(new, (w_gate, w_up, w_down))])


def solution(mesh):
    fine = Mesh(mesh.devices.reshape(tuple(SIZES.values())), tuple(SIZES))
    in_specs = (
        P(None, EXPERT_AXES, DP_AXES),
        P(None, EXPERT_AXES, None),
        P(None, EXPERT_AXES, None),
        P(),
        P(),
        P(EXPERT_AXES, None, DP_AXES),
        P(EXPERT_AXES, None, DP_AXES),
        P(EXPERT_AXES, DP_AXES, None),
    )
    out_specs = (
        P(None, EXPERT_AXES, DP_AXES),
        P(EXPERT_AXES),
        P(EXPERT_AXES, None, DP_AXES),
        P(EXPERT_AXES, None, DP_AXES),
        P(EXPERT_AXES, DP_AXES, None),
    )
    return jax.shard_map(on_device, mesh=fine, in_specs=in_specs, out_specs=out_specs, check_vma=False)
```
